1024 devices in a mesh: sec: 4 (over y_lo, core), row: 8 (over x), col: 32 (over y_hi, z).
Axes of the slice: x: 8, y: 8 (y_hi: 4, y_lo: 2; y = y_hi * 2 + y_lo), z: 8, core: 2. Of those that a mesh axis runs over, the one named last changes fastest.
Arguments:
- gas_field: float32 [4, 32, 64, 1024], P('sec', 'row', 'col'), may hold values from -6 to 6
- parcel_state: float32 [4, 1048576], P('sec', ('row', 'col')), may hold values from -6 to 6
- parcel_mass: float32 [1048576], P(('row', 'col')), may hold values from 0.5 to 2
- base_time: float32 [1048576], P(('row', 'col')), may hold values from 0.5 to 4
- evap_rate: float32 [1048576], P(('row', 'col')), may hold values from 0.1 to 1
- slot_blocks: int32 [256, 32, 4], P(('row', 'col')), may hold values from 0 to 63
- parcel_block_slot: int32 [1048576], P(('row', 'col')), may hold values from 0 to 127
- parcel_cell: int32 [1048576], P(('row', 'col')), may hold values from 0 to 127
- parcel_count: int32 [256], P(('row', 'col')), may hold values from 1024 to 4096, as said below
Outputs:
- gas_out: float32 [4, 32, 64, 1024], P('sec', 'row', 'col')
- parcel_out: float32 [4, 1048576], P('sec', ('row', 'col'))
- mass_out: float32 [1048576], P(('row', 'col'))
The draws below stay inside these ranges and needn't reach their ends.
Inputs may be any that keep to these rules, and one draw needn't show every extreme that they name: `slot_blocks`: local block indices of the owner; repeats allowed. `parcel_count`: some parcel block is full, with exactly 4096 live rows.
All inputs are finite; a program needn't handle non-finite values.
Results may differ from the reference program's by a relative error of at most 0.0015.
Values may be sent and summed in bfloat16 or wider, within the bound.
No kernel may reach another device: no remote copies, remote signals or barrier semaphores. Data moves between devices by JAX's collectives and lax.ppermute only.
A program may use at most 32 MiB of HBM per device.

```python
import math
import jax
import jax.numpy as jnp
import numpy as np
from jax import lax

CX = 4
CY = 2
NZ = 1024
P_DEV = 4096
K_SLOTS = 4
ITERS = 4
NX = 32
NY = 64
NBLK = 64
BLOCK_SLOTS = 128
SPRAY_DEVS = 256
PARCEL_ROWS = 1048576
N_ROW = 8
N_COL = 32


def draw_parcel_count(key, part):
    counts = jax.random.randint(jax.random.fold_in(key, 11), (SPRAY_DEVS,), P_DEV // 4, P_DEV + 1)
    chosen = jax.random.randint(jax.random.fold_in(key, 12), (), 0, SPRAY_DEVS)
    return jnp.where(jnp.arange(SPRAY_DEVS) == chosen, P_DEV, counts).astype(jnp.int32)


def set_ends(values, key, low, high):
    extent = values.shape
    place = [jax.random.randint(jax.random.fold_in(key, axis), (), 0, extent[axis]) for axis in range(len(extent))]
    values = values.at[tuple(place)].set(low)
    longest = extent.index(max(extent))
    place[longest] = (place[longest] + 1) % extent[longest]
    return values.at[tuple(place)].set(high)


def level_of(stream_key, dims, cuts, smallest, largest):
    factor_of, own = 1.0, jax.random.fold_in(stream_key, 6)
    for axis_at, shards_of in cuts:
        steps = jnp.exp(jax.random.uniform(jax.random.fold_in(own, axis_at), (shards_of,), jnp.float32, smallest / len(cuts), largest / len(cuts)))
        factor_of = factor_of * jnp.repeat(steps, dims[axis_at] // shards_of).reshape([-1 if axis == axis_at else 1 for axis in range(len(dims))])
    return factor_of


def cumulative_ranks(count, lean):
    loads = [(1 << 20) // math.isqrt(grade ** lean) + 1 for grade in range(1, count + 1)]
    scale = 1 + sum(loads) // (1 << 30)
    return np.cumsum(np.array([max(1, weight // scale) for weight in loads]))


def skewed_ids(stream_key, dims, count, slope):
    listing = cumulative_ranks(count, slope)
    pick = jax.random.randint(jax.random.fold_in(stream_key, 1), dims, 0, int(listing[count - 1]))
    grade = jnp.searchsorted(jnp.asarray(listing, jnp.int32), pick, side="right")
    return jax.random.permutation(jax.random.fold_in(stream_key, 2), count)[grade].astype(jnp.int32)


def noise(own_key, dims, width, most, shards=(), kind=jnp.bfloat16):
    result = width * jax.random.normal(own_key, dims, jnp.float32)
    if shards:
        result = result * level_of(own_key, dims, shards, -0.22, 0.18)
    return jnp.clip(result, -most, most).astype(kind)


def setup_inputs(seed: int = 0) -> dict:
    arg_keys = jax.random.split(jax.random.key(seed), 10)
    gas_field = noise(arg_keys[0], (4, NX, NY, NZ), 1.0, 6.0, ((0, 4), (1, 8), (2, 32)), jnp.float32)
    parcel_state = noise(arg_keys[1], (4, PARCEL_ROWS), 1.0, 6.0, ((0, 4), (1, 256)), jnp.float32)
    parcel_mass = jnp.clip(jnp.exp(math.log(2.0) - 1.3862944 * jax.random.uniform(arg_keys[2], (PARCEL_ROWS,), jnp.float32) ** level_of(arg_keys[2], (PARCEL_ROWS,), ((0, 256),), -0.2, 0.2)), 0.5, 2.0)
    base_time = jnp.clip(jnp.exp(math.log(4.0) - 2.0794415 * jax.random.uniform(arg_keys[3], (PARCEL_ROWS,), jnp.float32) ** level_of(arg_keys[3], (PARCEL_ROWS,), ((0, 256),), -0.2, 0.2)), 0.5, 4.0)
    evap_rate = jnp.clip(jnp.exp(math.log(1.0) - 2.3025851 * jax.random.uniform(arg_keys[4], (PARCEL_ROWS,), jnp.float32) ** level_of(arg_keys[4], (PARCEL_ROWS,), ((0, 256),), -0.2, 0.2)), 0.1, 1.0)
    slot_blocks = set_ends(skewed_ids(arg_keys[5], (SPRAY_DEVS, N_COL, K_SLOTS), NBLK, 2), jax.random.fold_in(arg_keys[5], 3), 0, NBLK - 1).astype(jnp.int32)
    parcel_block_slot = set_ends(skewed_ids(arg_keys[6], (PARCEL_ROWS,), BLOCK_SLOTS, 1), jax.random.fold_in(arg_keys[6], 3), 0, BLOCK_SLOTS - 1).astype(jnp.int32)
    parcel_cell = set_ends(jax.random.randint(arg_keys[7], (PARCEL_ROWS,), 0, 128), jax.random.fold_in(arg_keys[7], 1), 0, 127).astype(jnp.int32)
    parcel_count = draw_parcel_count(jax.random.fold_in(arg_keys[9], 71), 0)
    return {"gas_field": gas_field, "parcel_state": parcel_state, "parcel_mass": parcel_mass, "base_time": base_time, "evap_rate": evap_rate, "slot_blocks": slot_blocks, "parcel_block_slot": parcel_block_slot, "parcel_cell": parcel_cell, "parcel_count": parcel_count}


LATENT = 2.0
DEPOSIT_MODE = 0.5
ADVECT = 0.3
DIFFUSE = 0.2


def transport(current_gas):
    left = jnp.concatenate([current_gas[..., :1], current_gas[..., :-1]], axis=-1)
    right = jnp.concatenate([current_gas[..., 1:], current_gas[..., -1:]], axis=-1)
    return current_gas + ADVECT * (left - current_gas) + DIFFUSE * (right - 2.0 * current_gas + left)


def reference(gas_field, parcel_state, parcel_mass, base_time, evap_rate, slot_blocks, parcel_block_slot, parcel_cell, parcel_count):
    nparcel = P_DEV * N_ROW * N_COL
    indices = jnp.arange(nparcel, dtype=jnp.int32)
    owner_dev = indices // P_DEV
    local_row = indices % P_DEV
    row_block = owner_dev // N_COL
    owner_col = parcel_block_slot // K_SLOTS
    slot_pos = parcel_block_slot % K_SLOTS
    block_index = slot_blocks[owner_dev, owner_col, slot_pos]
    local_cell = block_index * 128 + parcel_cell
    x_cell = row_block * CX + local_cell // (CY * NZ)
    y_cell = owner_col * CY + (local_cell // NZ) % CY
    z_cell = local_cell % NZ
    flat_pos = ((x_cell * NY + y_cell) * NZ + z_cell).astype(jnp.int32)
    active = local_row < parcel_count[owner_dev]
    heat_factor = jnp.array([1.0, 1.0, 1.0, 1.5], jnp.float32)[:, None]
    latent = jnp.array([0.0, 0.0, 0.0, LATENT], jnp.float32)[:, None]
    grid_shape = (4, NX, NY, NZ)
    current_gas = gas_field
    drop_state = parcel_state
    drop_mass = parcel_mass
    for substep in range(ITERS):
        rounded = current_gas.astype(jnp.bfloat16)
        rounded = lax.optimization_barrier(rounded)
        sent_gas = rounded.astype(jnp.float32).reshape(4, NX * NY * NZ)
        sampled_draws = sent_gas[:, flat_pos]
        evap_now = evap_rate * jax.nn.sigmoid(sampled_draws[3] - drop_state[3])
        updated_mass = jnp.where(active, drop_mass * jnp.exp(-evap_now), drop_mass)
        response_time = base_time * jnp.exp(jnp.log(drop_mass) * (2.0 / 3.0)) * heat_factor
        relaxed = sampled_draws + (drop_state - sampled_draws) * jnp.exp(-1.0 / response_time)
        new_state = jnp.where(active[None, :], relaxed, drop_state)
        source = drop_mass * drop_state - updated_mass * new_state - latent * (drop_mass - updated_mass)
        deposit = jnp.zeros((4, NX * NY * NZ), jnp.float32).at[:, flat_pos].add(source)
        current_gas = transport(current_gas) + DEPOSIT_MODE * deposit.reshape(grid_shape)
        drop_state = new_state
        drop_mass = updated_mass
    return current_gas, drop_state, drop_mass
```

```python
import functools

import jax
import jax.numpy as jnp
from jax import lax
from jax.experimental import pallas as pl
from jax.experimental.pallas import tpu as pltpu
from jax.sharding import PartitionSpec as P

ITERS = 4
LATENT = 2.0
DEPOSIT_MODE = 0.5
ADVECT = 0.3
DIFFUSE = 0.2
LANES = 128
HALF = 64
VMEM_LIMIT = 32 * 1024 * 1024

F32 = jnp.float32
BF16 = jnp.bfloat16


def iota(shape, axis):
    return lax.broadcasted_iota(jnp.int32, shape, axis)


def dot(left_side, right_side, left_axis=1, right_axis=0):
    return lax.dot_general(
        left_side,
        right_side,
        (((left_axis,), (right_axis,)), ((), ())),
        preferred_element_type=F32,
    )


def halves(values):
    high = values.astype(BF16)
    return high, (values - high.astype(F32)).astype(BF16)


def split_pair(rows):
    tiles = rows.reshape(rows.shape[0] // 16, 2, 8, LANES)
    even, odd = tiles[:, 0], tiles[:, 1]
    low = iota(even.shape, 1) < 4
    first = jnp.where(low, even, pltpu.roll(odd, 4, 1))
    second = jnp.where(low, pltpu.roll(even, 4, 1), odd)
    flat = (rows.shape[0] // 2, LANES)
    return first.reshape(flat), second.reshape(flat)


def merge_pair(first, second):
    shape = (first.shape[0] // 8, 8, LANES)
    first, second = first.reshape(shape), second.reshape(shape)
    low = iota(shape, 1) < 4
    even = jnp.where(low, first, pltpu.roll(second, 4, 1))
    odd = jnp.where(low, pltpu.roll(first, 4, 1), second)
    return jnp.stack([even, odd], axis=1).reshape(2 * shape[0] * 8, LANES)


def pick_kernel(wanted_ref, gas_ref, pick_ref, place_ref, send_ref):
    wanted = wanted_ref[...].astype(F32).astype(jnp.int32)
    pick = (wanted == iota(wanted.shape, 1)).astype(F32)
    pick_ref[...] = pick.astype(BF16)
    place_ref[...] = pick.T.astype(BF16)
    send_ref[...] = dot(pick.astype(BF16), gas_ref[...].astype(BF16)).astype(BF16)


def gas_kernel(per_pencil, source_ref, gas_ref, pick_ref, place_ref, gas_out, send_ref=None):
    high, low = halves(source_ref[...])
    place = place_ref[...]
    deposit = dot(place, high) + dot(place, low)
    gas = gas_ref[...]
    rows = gas.shape[0]
    block = iota(gas.shape, 0) % per_pencil
    lane = iota(gas.shape, 1)
    to_right = pltpu.roll(gas, 1, 1)
    to_left = pltpu.roll(gas, LANES - 1, 1)
    left = jnp.where(
        lane == 0, jnp.where(block == 0, gas, pltpu.roll(to_right, 1, 0)), to_right
    )
    right = jnp.where(
        lane == LANES - 1,
        jnp.where(block == per_pencil - 1, gas, pltpu.roll(to_left, rows - 1, 0)),
        to_left,
    )
    moved = gas + ADVECT * (left - gas) + DIFFUSE * (right - 2.0 * gas + left)
    new_gas = moved + DEPOSIT_MODE * deposit
    gas_out[...] = new_gas
    if send_ref is not None:
        send_ref[...] = dot(pick_ref[...], new_gas.astype(BF16)).astype(BF16)


def parcel_kernel(
    chunk,
    count_ref,
    coef_ref,
    recv_ref,
    drop_ref,
    mass_ref,
    base_ref,
    evap_ref,
    slot_ref,
    cell_ref,
    drop_out,
    mass_out,
    send_ref,
    seen_ref,
    part_ref,
):
    lines = mass_ref.shape[0]
    slots = recv_ref.shape[0] // 2
    width = chunk * LANES

    def fold(values):
        turned = values.T
        return jnp.concatenate([turned[:HALF], turned[HALF:]], axis=1)

    own, temp = split_pair(recv_ref[...].astype(F32))
    table = jnp.concatenate([fold(own), fold(temp)], axis=0).astype(BF16)
    cell = cell_ref[...]
    upper = cell // HALF
    part_ref[4] = (slot_ref[...] + slots * upper).astype(F32)
    part_ref[5] = (cell - HALF * upper).astype(F32)

    def packed(ref, start):
        row = jnp.concatenate([ref[start + i : start + i + 1, :] for i in range(chunk)], axis=1)
        return jnp.broadcast_to(row, (16, width)).astype(BF16)[None]

    def index(count):
        shape = (count // 16, 16, width)
        return (iota(shape, 0) * 16 + iota(shape, 1)).astype(F32).astype(BF16)

    slot_index, cell_index = index(2 * slots), index(HALF)
    one, zero = jnp.ones((), BF16), jnp.zeros((), BF16)

    def masks(start):
        hot = jnp.where(slot_index == packed(part_ref.at[4], start), one, zero)
        return hot.reshape(2 * slots, width), cell_index == packed(part_ref.at[5], start)

    for start in range(0, lines, chunk):
        hot, here = masks(start)
        values = dot(table, hot).astype(BF16).reshape(2, HALF // 16, 16, width)
        for quantity in range(2):
            kept = jnp.where(here, values[quantity], zero)
            total = kept[0]
            for i in range(1, HALF // 16):
                total = total + kept[i]
            seen = jnp.sum(total.astype(F32), axis=0, keepdims=True)
            for i in range(chunk):
                seen_ref[quantity, start + i : start + i + 1, :] = seen[:, i * LANES : (i + 1) * LANES]

    shape = mass_ref.shape
    active = iota(shape, 0) * LANES + iota(shape, 1) < count_ref[0]
    mass = mass_ref[...]
    evap_now = evap_ref[...] * jax.nn.sigmoid(seen_ref[1] - drop_ref[1])
    new_mass = jnp.where(active, mass * jnp.exp(-evap_now), mass)
    mass_out[...] = new_mass
    unit_time = base_ref[...] * jnp.exp(jnp.log(mass) * (2.0 / 3.0))
    for quantity in range(2):
        heat = coef_ref[0] if quantity == 0 else 1.5
        latent = coef_ref[1] if quantity == 0 else LATENT
        seen, drop = seen_ref[quantity], drop_ref[quantity]
        relaxed = seen + (drop - seen) * jnp.exp(-1.0 / (unit_time * heat))
        new_drop = jnp.where(active, relaxed, drop)
        drop_out[quantity] = new_drop
        source = mass * drop - new_mass * new_drop - latent * (mass - new_mass)
        high = source.astype(BF16).astype(F32)
        part_ref[quantity] = high
        part_ref[2 + quantity] = source - high

    total = jnp.zeros((2 * slots, 4 * HALF), F32)
    for start in range(0, lines, chunk):
        hot, here = masks(start)
        parts = [
            jnp.where(here, packed(part_ref.at[i], start), zero).reshape(HALF, width)
            for i in range(4)
        ]
        total += dot(hot, jnp.concatenate(parts, axis=0), 1, 1)
    total = total[:, :LANES] + total[:, LANES:]
    lower, upper = total[:slots], total[slots:]
    left = iota(lower.shape, 1) < HALF
    first = jnp.where(left, lower, pltpu.roll(upper, HALF, 1))
    second = jnp.where(left, pltpu.roll(lower, HALF, 1), upper)
    send_ref[...] = merge_pair(first, second)


def call(body, out_shape, in_specs, **more):
    return pl.pallas_call(
        body,
        out_shape=out_shape,
        in_specs=in_specs,
        out_specs=jax.tree.map(lambda _: pl.BlockSpec(memory_space=pltpu.VMEM), out_shape),
        compiler_params=pltpu.CompilerParams(vmem_limit_bytes=VMEM_LIMIT),
        **more,
    )


def exchange(rows, peers):
    shape = (peers, rows.shape[0] // peers, LANES)
    return lax.all_to_all(rows.reshape(shape), "col", 0, 0, tiled=True).reshape(rows.shape)


def shards(
    gas_field,
    parcel_state,
    parcel_mass,
    base_time,
    evap_rate,
    slot_blocks,
    parcel_block_slot,
    parcel_cell,
    parcel_count,
):
    cells = gas_field.shape[1:]
    blocks = cells[0] * cells[1] * cells[2] // LANES
    per_pencil = cells[2] // LANES
    peers, per_peer = slot_blocks.shape[1:]
    lines = parcel_mass.shape[0] // LANES
    rows = 2 * peers * per_peer
    section = lax.axis_index("sec")
    coef = jnp.stack(
        [jnp.where(section == 3, 1.5, 1.0), jnp.where(section == 3, LATENT, 0.0)]
    ).astype(F32)

    own_gas = gas_field.reshape(blocks, LANES)
    own_drop = parcel_state.reshape(lines, LANES)
    together = lax.all_gather(jnp.concatenate([own_gas, own_drop], axis=0), "sec")[3]
    gas = jnp.concatenate([own_gas, together[:blocks]], axis=0)
    drop = jnp.stack([own_drop, together[blocks:]])
    mass = parcel_mass.reshape(lines, LANES)
    base = base_time.reshape(lines, LANES)
    evap = evap_rate.reshape(lines, LANES)
    slot = parcel_block_slot.reshape(lines, LANES)
    cell = parcel_cell.reshape(lines, LANES)

    wanted = slot_blocks[0][:, None, :] + blocks * jnp.arange(2, dtype=jnp.int32)[None, :, None]
    wanted = jnp.broadcast_to(wanted.reshape(rows, 1), (rows, LANES)).astype(BF16)
    wanted = exchange(wanted, peers)

    vmem = pl.BlockSpec(memory_space=pltpu.VMEM)
    smem = pl.BlockSpec(memory_space=pltpu.SMEM)

    def shape(dims, kind=F32):
        return jax.ShapeDtypeStruct(dims, kind)

    gas_shape = shape((2 * blocks, LANES))
    send_shape = shape((rows, LANES), BF16)
    pick, place, send = call(
        pick_kernel,
        (shape((rows, 2 * blocks), BF16), shape((2 * blocks, rows), BF16), send_shape),
        [vmem] * 2,
    )(wanted, gas)
    for substep in range(ITERS):
        recv = exchange(send, peers)
        drop, mass, source = call(
            functools.partial(parcel_kernel, 4),
            (shape((2, lines, LANES)), shape((lines, LANES)), shape((rows, LANES))),
            [smem] * 2 + [vmem] * 7,
            scratch_shapes=[pltpu.VMEM((2, lines, LANES), F32), pltpu.VMEM((6, lines, LANES), F32)],
        )(parcel_count, coef, recv, drop, mass, base, evap, slot, cell)
        source = exchange(source, peers)
        last = substep == ITERS - 1
        result = call(
            functools.partial(gas_kernel, per_pencil),
            (gas_shape,) if last else (gas_shape, send_shape),
            [vmem] * 4,
        )(source, gas, pick, place)
        gas = result[0]
        if not last:
            send = result[1]
    return (gas[:blocks].reshape(gas_field.shape), drop[:1].reshape(parcel_state.shape), mass.reshape(parcel_mass.shape))


def solution(mesh):
    return jax.shard_map(
        shards,
        mesh=mesh,
        in_specs=(
            P("sec", "row", "col", None),
            P("sec", ("row", "col")),
            P(("row", "col")),
            P(("row", "col")),
            P(("row", "col")),
            P(("row", "col"), None, None),
            P(("row", "col")),
            P(("row", "col")),
            P(("row", "col")),
        ),
        out_specs=(P("sec", "row", "col", None), P("sec", ("row", "col")), P(("row", "col"))),
        check_vma=False,
    )
```

```python
import functools

import jax
import jax.numpy as jnp
from jax import lax
from jax.experimental import pallas as pl
from jax.experimental.pallas import tpu as pltpu
from jax.sharding import Mesh
from jax.sharding import PartitionSpec as P

ITERS = 4
LATENT = 2.0
DEPOSIT_MODE = 0.5
ADVECT = 0.3
DIFFUSE = 0.2
LANES = 128
HALF = 64
GROUP = ("sec", "near")
VMEM_LIMIT = 32 * 1024 * 1024

F32 = jnp.float32
BF16 = jnp.bfloat16


def iota(shape, axis):
    return lax.broadcasted_iota(jnp.int32, shape, axis)


def dot(left_side, right_side, left_axis=1, right_axis=0):
    return lax.dot_general(
        left_side,
        right_side,
        (((left_axis,), (right_axis,)), ((), ())),
        preferred_element_type=F32,
    )


def halves(values):
    high = values.astype(BF16)
    return high, (values - high.astype(F32)).astype(BF16)


def split_pair(rows):
    tiles = rows.reshape(rows.shape[0] // 16, 2, 8, LANES)
    even, odd = tiles[:, 0], tiles[:, 1]
    low = iota(even.shape, 1) < 4
    first = jnp.where(low, even, pltpu.roll(odd, 4, 1))
    second = jnp.where(low, pltpu.roll(even, 4, 1), odd)
    flat = (rows.shape[0] // 2, LANES)
    return first.reshape(flat), second.reshape(flat)


def merge_pair(first, second):
    shape = (first.shape[0] // 8, 8, LANES)
    first, second = first.reshape(shape), second.reshape(shape)
    low = iota(shape, 1) < 4
    even = jnp.where(low, first, pltpu.roll(second, 4, 1))
    odd = jnp.where(low, pltpu.roll(first, 4, 1), second)
    return jnp.stack([even, odd], axis=1).reshape(2 * shape[0] * 8, LANES)


def pick_kernel(wanted_ref, gas_ref, pick_ref, place_ref, send_ref):
    wanted = wanted_ref[...].astype(F32).astype(jnp.int32)
    pick = (wanted == iota(wanted.shape, 1)).astype(F32)
    pick_ref[...] = pick.astype(BF16)
    place_ref[...] = pick.T.astype(BF16)
    send_ref[...] = dot(pick.astype(BF16), gas_ref[...].astype(BF16)).astype(BF16)


def gas_kernel(per_pencil, source_ref, gas_ref, pick_ref, place_ref, gas_out, send_ref=None):
    high, low = halves(source_ref[...])
    place = place_ref[...]
    deposit = dot(place, high) + dot(place, low)
    gas = gas_ref[...]
    rows = gas.shape[0]
    block = iota(gas.shape, 0) % per_pencil
    lane = iota(gas.shape, 1)
    to_right = pltpu.roll(gas, 1, 1)
    to_left = pltpu.roll(gas, LANES - 1, 1)
    left = jnp.where(
        lane == 0, jnp.where(block == 0, gas, pltpu.roll(to_right, 1, 0)), to_right
    )
    right = jnp.where(
        lane == LANES - 1,
        jnp.where(block == per_pencil - 1, gas, pltpu.roll(to_left, rows - 1, 0)),
        to_left,
    )
    moved = gas + ADVECT * (left - gas) + DIFFUSE * (right - 2.0 * gas + left)
    new_gas = moved + DEPOSIT_MODE * deposit
    gas_out[...] = new_gas
    if send_ref is not None:
        send_ref[...] = dot(pick_ref[...], new_gas.astype(BF16)).astype(BF16)


def parcel_kernel(
    chunk,
    count_ref,
    coef_ref,
    recv_ref,
    drop_ref,
    mass_ref,
    base_ref,
    evap_ref,
    slot_ref,
    cell_ref,
    drop_out,
    mass_out,
    send_ref,
    seen_ref,
    part_ref,
):
    lines = mass_ref.shape[0]
    slots = recv_ref.shape[0] // 2
    width = chunk * LANES

    def fold(values):
        turned = values.T
        return jnp.concatenate([turned[:HALF], turned[HALF:]], axis=1)

    own, temp = split_pair(recv_ref[...].astype(F32))
    table = jnp.concatenate([fold(own), fold(temp)], axis=0).astype(BF16)
    def packed(ref, start):
        row = jnp.concatenate([ref[start + i : start + i + 1, :] for i in range(chunk)], axis=1)
        return jnp.broadcast_to(row, (16, width)).astype(BF16)[None]

    def index(count):
        shape = (count // 16, 16, width)
        return (iota(shape, 0) * 16 + iota(shape, 1)).astype(F32).astype(BF16)

    slot_index, cell_index = index(2 * slots), index(HALF)
    one, zero = jnp.ones((), BF16), jnp.zeros((), BF16)

    def masks(start):
        hot = jnp.where(slot_index == packed(slot_ref, start), one, zero)
        return hot.reshape(2 * slots, width), cell_index == packed(cell_ref, start)

    for start in range(0, lines, chunk):
        hot, here = masks(start)
        values = dot(table, hot).astype(BF16).reshape(2, HALF // 16, 16, width)
        for quantity in range(2):
            kept = jnp.where(here, values[quantity], zero)
            total = kept[0]
            for i in range(1, HALF // 16):
                total = total + kept[i]
            seen = jnp.sum(total.astype(F32), axis=0, keepdims=True)
            for i in range(chunk):
                seen_ref[quantity, start + i : start + i + 1, :] = seen[:, i * LANES : (i + 1) * LANES]

    shape = mass_ref.shape
    active = iota(shape, 0) * LANES + iota(shape, 1) < count_ref[0]
    mass = mass_ref[...]
    evap_now = evap_ref[...] * jax.nn.sigmoid(seen_ref[1] - drop_ref[1])
    new_mass = jnp.where(active, mass * jnp.exp(-evap_now), mass)
    mass_out[...] = new_mass
    unit_time = base_ref[...] * jnp.exp(jnp.log(mass) * (2.0 / 3.0))
    for quantity in range(2):
        heat = coef_ref[0] if quantity == 0 else 1.5
        latent = coef_ref[1] if quantity == 0 else LATENT
        seen, drop = seen_ref[quantity], drop_ref[quantity]
        relaxed = seen + (drop - seen) * jnp.exp(-1.0 / (unit_time * heat))
        new_drop = jnp.where(active, relaxed, drop)
        drop_out[quantity] = new_drop
        source = mass * drop - new_mass * new_drop - latent * (mass - new_mass)
        high = source.astype(BF16).astype(F32)
        part_ref[quantity] = high
        part_ref[2 + quantity] = source - high

    total = jnp.zeros((2 * slots, 4 * HALF), F32)
    for start in range(0, lines, chunk):
        hot, here = masks(start)
        parts = [
            jnp.where(here, packed(part_ref.at[i], start), zero).reshape(HALF, width)
            for i in range(4)
        ]
        total += dot(hot, jnp.concatenate(parts, axis=0), 1, 1)
    total = total[:, :LANES] + total[:, LANES:]
    lower, upper = total[:slots], total[slots:]
    left = iota(lower.shape, 1) < HALF
    first = jnp.where(left, lower, pltpu.roll(upper, HALF, 1))
    second = jnp.where(left, pltpu.roll(lower, HALF, 1), upper)
    send_ref[...] = merge_pair(first, second)


def call(body, out_shape, in_specs, **more):
    return pl.pallas_call(
        body,
        out_shape=out_shape,
        in_specs=in_specs,
        out_specs=jax.tree.map(lambda _: pl.BlockSpec(memory_space=pltpu.VMEM), out_shape),
        compiler_params=pltpu.CompilerParams(vmem_limit_bytes=VMEM_LIMIT),
        **more,
    )


def exchange(rows, peers):
    shape = (peers, rows.shape[0] // peers, LANES)
    return lax.all_to_all(rows.reshape(shape), GROUP, 0, 0, tiled=True).reshape(rows.shape)


def swap(values):
    side = lax.axis_size("sec")
    pairs = [(i * side + j, j * side + i) for i in range(side) for j in range(side)]
    return lax.ppermute(values, ("sec", "far"), pairs)


def shards(
    gas_field,
    parcel_state,
    parcel_mass,
    base_time,
    evap_rate,
    slot_blocks,
    parcel_block_slot,
    parcel_cell,
    parcel_count,
):
    cells = gas_field.shape[1:]
    blocks = cells[0] * cells[1] * cells[2] // LANES
    per_pencil = cells[2] // LANES
    peers, per_peer = slot_blocks.shape[1:]
    slots = peers * per_peer
    lines = parcel_mass.shape[0] // LANES
    rows = 2 * slots

    quantity = lax.axis_index("far")
    coef = jnp.stack(
        [jnp.where(quantity == 3, 1.5, 1.0), jnp.where(quantity == 3, LATENT, 0.0)]
    ).astype(F32)

    small = jnp.concatenate(
        [slot_blocks.reshape(1, slots), jnp.broadcast_to(parcel_count[:, None], (1, slots))]
    )
    small = swap(small.astype(F32)).astype(jnp.int32)
    block_lists, count = small[0].reshape(peers, per_peer), small[1, :1]

    own_gas = gas_field.reshape(blocks, LANES)
    own_drop = parcel_state.reshape(lines, LANES)
    together = lax.all_gather(jnp.concatenate([own_gas, own_drop], axis=0), "sec")[3]
    gas = swap(jnp.concatenate([own_gas, together[:blocks]], axis=0))
    upper = parcel_cell // HALF
    parcels = [
        own_drop,
        together[blocks:],
        parcel_mass,
        base_time,
        evap_rate,
        (parcel_block_slot + slots * upper).astype(F32),
        (parcel_cell - HALF * upper).astype(F32),
    ]
    parcels = swap(jnp.stack([part.reshape(lines, LANES) for part in parcels]))
    drop = parcels[:2]
    mass, base, evap, slot, cell = (parcels[i] for i in range(2, 7))

    wanted = block_lists[:, None, :] + blocks * jnp.arange(2, dtype=jnp.int32)[None, :, None]
    wanted = jnp.broadcast_to(wanted.reshape(rows, 1), (rows, LANES)).astype(BF16)
    wanted = exchange(wanted, peers)

    vmem = pl.BlockSpec(memory_space=pltpu.VMEM)
    smem = pl.BlockSpec(memory_space=pltpu.SMEM)

    def shape(dims, kind=F32):
        return jax.ShapeDtypeStruct(dims, kind)

    gas_shape = shape((2 * blocks, LANES))
    send_shape = shape((rows, LANES), BF16)
    pick, place, send = call(
        pick_kernel,
        (shape((rows, 2 * blocks), BF16), shape((2 * blocks, rows), BF16), send_shape),
        [vmem] * 2,
    )(wanted, gas)
    for substep in range(ITERS):
        recv = exchange(send, peers)
        drop, mass, source = call(
            functools.partial(parcel_kernel, 4),
            (shape((2, lines, LANES)), shape((lines, LANES)), shape((rows, LANES))),
            [smem] * 2 + [vmem] * 7,
            scratch_shapes=[pltpu.VMEM((2, lines, LANES), F32), pltpu.VMEM((4, lines, LANES), F32)],
        )(count, coef, recv, drop, mass, base, evap, slot, cell)
        source = exchange(source, peers)
        last = substep == ITERS - 1
        result = call(
            functools.partial(gas_kernel, per_pencil),
            (gas_shape,) if last else (gas_shape, send_shape),
            [vmem] * 4,
        )(source, gas, pick, place)
        gas = result[0]
        if not last:
            send = result[1]
    parcels = swap(jnp.stack([drop[0], mass]))
    gas = swap(gas[:blocks])
    return (
        gas.reshape(gas_field.shape),
        parcels[0].reshape(parcel_state.shape),
        parcels[1].reshape(parcel_mass.shape),
    )


def solution(mesh):
    sec, row, col = (mesh.shape[name] for name in ("sec", "row", "col"))
    split = Mesh(mesh.devices.reshape(sec, row, sec, col // sec), ("sec", "row", "far", "near"))
    place = P(("row", "far", "near"))
    return jax.shard_map(
        shards,
        mesh=split,
        in_specs=(
            P("sec", "row", ("far", "near"), None),
            P("sec", ("row", "far", "near")),
            place,
            place,
            place,
            P(("row", "far", "near"), None, None),
            place,
            place,
            place,
        ),
        out_specs=(
            P("sec", "row", ("far", "near"), None),
            P("sec", ("row", "far", "near")),
            place,
        ),
        check_vma=False,
    )
```

```python
import functools

import jax
import jax.numpy as jnp
from jax import lax
from jax.experimental import pallas as pl
from jax.experimental.pallas import tpu as pltpu
from jax.sharding import Mesh
from jax.sharding import PartitionSpec as P

ITERS = 4
LATENT = 2.0
DEPOSIT_MODE = 0.5
ADVECT = 0.3
DIFFUSE = 0.2
LANES = 128
HALF = 64
GROUP = ("sec", "near")
OWN, MASS, TEMP, BASE, EVAP, SLOT, CELL = range(7)
VMEM_LIMIT = 32 * 1024 * 1024

F32 = jnp.float32
BF16 = jnp.bfloat16


def iota(shape, axis):
    return lax.broadcasted_iota(jnp.int32, shape, axis)


def dot(left_side, right_side, left_axis=1, right_axis=0):
    return lax.dot_general(
        left_side,
        right_side,
        (((left_axis,), (right_axis,)), ((), ())),
        preferred_element_type=F32,
    )


def halves(values):
    high = values.astype(BF16)
    return high, (values - high.astype(F32)).astype(BF16)


def split_pair(rows):
    tiles = rows.reshape(rows.shape[0] // 16, 2, 8, LANES)
    even, odd = tiles[:, 0], tiles[:, 1]
    low = iota(even.shape, 1) < 4
    first = jnp.where(low, even, pltpu.roll(odd, 4, 1))
    second = jnp.where(low, pltpu.roll(even, 4, 1), odd)
    flat = (rows.shape[0] // 2, LANES)
    return first.reshape(flat), second.reshape(flat)


def merge_pair(first, second):
    shape = (first.shape[0] // 8, 8, LANES)
    first, second = first.reshape(shape), second.reshape(shape)
    low = iota(shape, 1) < 4
    even = jnp.where(low, first, pltpu.roll(second, 4, 1))
    odd = jnp.where(low, pltpu.roll(first, 4, 1), second)
    return jnp.stack([even, odd], axis=1).reshape(2 * shape[0] * 8, LANES)


def order_kernel(per_peer, pencils, per_pencil, blocks, list_ref, rows_ref):
    block = list_ref[0]
    first = block // (pencils * per_pencil)
    rest = block - first * (pencils * per_pencil)
    pencil = rest // per_pencil
    place = first * (pencils * per_pencil) + (rest - pencil * per_pencil) * pencils + pencil
    rows, peers = rows_ref.shape[0], block.shape[0]
    each = rows // peers
    owner = (iota((rows, peers), 0) // each == iota((rows, peers), 1)).astype(BF16)
    spread = dot(owner, place.astype(F32).astype(BF16))
    within = iota(spread.shape, 0) % each
    kept = jnp.where(within % per_peer == iota(spread.shape, 1), spread, 0.0)
    value = jnp.sum(kept, axis=1, keepdims=True)
    value = value + (blocks * (within[:, :1] // per_peer)).astype(F32)
    rows_ref[...] = jnp.broadcast_to(value, rows_ref.shape).astype(BF16)


def pack_kernel(
    slots, count_ref, temp_ref, gas_ref, drop_ref, mass_ref, base_ref, evap_ref, slot_ref, cell_ref, out_ref
):
    blocks, lines = gas_ref.shape[0], mass_ref.shape[0]
    start = temp_ref.shape[0] - blocks - lines
    out_ref[:blocks] = gas_ref[...]
    out_ref[blocks : 2 * blocks] = temp_ref[start : start + blocks]

    def store(which, values):
        at = 2 * blocks + which * lines
        out_ref[at : at + lines] = values

    store(OWN, drop_ref[...])
    store(MASS, mass_ref[...])
    store(TEMP, temp_ref[start + blocks :])
    store(BASE, base_ref[...])
    store(EVAP, evap_ref[...])
    shape = mass_ref.shape
    active = iota(shape, 0) * LANES + iota(shape, 1) < count_ref[0]
    upper = cell_ref[...] // HALF
    store(SLOT, (slot_ref[...] + slots * upper).astype(F32))
    store(CELL, jnp.where(active, cell_ref[...] - HALF * upper, -1).astype(F32))


def pick_kernel(wanted_ref, pack_ref, pick_ref, place_ref, send_ref):
    wanted = wanted_ref[...].astype(F32).astype(jnp.int32)
    pick = (wanted == iota(wanted.shape, 1)).astype(F32)
    pick_ref[...] = pick.astype(BF16)
    place_ref[...] = pick.T.astype(BF16)
    gas = pack_ref[: wanted.shape[1]]
    send_ref[...] = dot(pick.astype(BF16), gas.astype(BF16)).astype(BF16)


def gas_kernel(stride, per_pencil, source_ref, gas_ref, pick_ref, place_ref, gas_out, send_ref=None):
    high, low = halves(source_ref[...])
    place = place_ref[...]
    deposit = dot(place, high) + dot(place, low)
    rows = place.shape[0]
    gas = gas_ref[:rows]
    block = iota(gas.shape, 0) // stride % per_pencil
    lane = iota(gas.shape, 1)
    to_right = pltpu.roll(gas, 1, 1)
    to_left = pltpu.roll(gas, LANES - 1, 1)
    left = jnp.where(
        lane == 0, jnp.where(block == 0, gas, pltpu.roll(to_right, stride, 0)), to_right
    )
    right = jnp.where(
        lane == LANES - 1,
        jnp.where(block == per_pencil - 1, gas, pltpu.roll(to_left, rows - stride, 0)),
        to_left,
    )
    moved = gas + ADVECT * (left - gas) + DIFFUSE * (right - 2.0 * gas + left)
    new_gas = moved + DEPOSIT_MODE * deposit
    gas_out[...] = new_gas[: gas_out.shape[0]]
    if send_ref is not None:
        send_ref[...] = dot(pick_ref[...], new_gas.astype(BF16)).astype(BF16)


def parcel_kernel(chunk, first, recv_ref, pack_ref, *refs):
    state_ref = None if first else refs[0]
    state_out, send_ref, seen_ref, part_ref = refs[-4:]
    lines = state_out.shape[1]
    base_row = pack_ref.shape[0] - 7 * lines
    slots = recv_ref.shape[0] // 2
    width = chunk * LANES

    def given(which):
        return pack_ref[base_row + which * lines : base_row + (which + 1) * lines]

    def held(which):
        return given(which) if first else state_ref[which]

    def fold(values):
        turned = values.T
        return jnp.concatenate([turned[:HALF], turned[HALF:]], axis=1)

    own, temp = split_pair(recv_ref[...].astype(F32))
    table = jnp.concatenate([fold(own), fold(temp)], axis=0).astype(BF16)

    def packed(ref, start):
        row = jnp.concatenate([ref[start + i : start + i + 1, :] for i in range(chunk)], axis=1)
        return jnp.broadcast_to(row, (16, width)).astype(BF16)[None]

    def index(count):
        shape = (count // 16, 16, width)
        return (iota(shape, 0) * 16 + iota(shape, 1)).astype(F32).astype(BF16)

    slot_index, cell_index = index(2 * slots), index(HALF)
    one, zero = jnp.ones((), BF16), jnp.zeros((), BF16)

    def masks(start):
        hot = jnp.where(slot_index == packed(pack_ref, base_row + SLOT * lines + start), one, zero)
        here = cell_index == packed(pack_ref, base_row + CELL * lines + start)
        return hot.reshape(2 * slots, width), here

    for start in range(0, lines, chunk):
        hot, here = masks(start)
        values = dot(table, hot).astype(BF16).reshape(2, HALF // 16, 16, width)
        for quantity in range(2):
            kept = jnp.where(here, values[quantity], zero)
            total = kept[0]
            for i in range(1, HALF // 16):
                total = total + kept[i]
            seen = jnp.sum(total.astype(F32), axis=0, keepdims=True)
            for i in range(chunk):
                seen_ref[quantity, start + i : start + i + 1, :] = seen[:, i * LANES : (i + 1) * LANES]

    hot_quantity = lax.axis_index("far") == 3
    own_heat = jnp.where(hot_quantity, 1.5, 1.0).astype(F32)
    own_latent = jnp.where(hot_quantity, LATENT, 0.0).astype(F32)
    active = given(CELL) >= 0.0
    mass = held(MASS)
    evap_now = given(EVAP) * jax.nn.sigmoid(seen_ref[1] - held(TEMP))
    new_mass = jnp.where(active, mass * jnp.exp(-evap_now), mass)
    state_out[MASS] = new_mass
    unit_time = given(BASE) * jnp.exp(jnp.log(mass) * (2.0 / 3.0))
    work = ((OWN, own_heat, own_latent), (TEMP, 1.5, LATENT))
    for quantity, (which, heat, latent) in enumerate(work):
        seen, drop = seen_ref[quantity], held(which)
        relaxed = seen + (drop - seen) * jnp.exp(-1.0 / (unit_time * heat))
        new_drop = jnp.where(active, relaxed, drop)
        if which < state_out.shape[0]:
            state_out[which] = new_drop
        source = mass * drop - new_mass * new_drop - latent * (mass - new_mass)
        high = source.astype(BF16).astype(F32)
        part_ref[quantity] = high
        part_ref[2 + quantity] = source - high

    total = jnp.zeros((2 * slots, 4 * HALF), F32)
    for start in range(0, lines, chunk):
        hot, here = masks(start)
        parts = [
            jnp.where(here, packed(part_ref.at[i], start), zero).reshape(HALF, width)
            for i in range(4)
        ]
        total += dot(hot, jnp.concatenate(parts, axis=0), 1, 1)
    total = total[:, :LANES] + total[:, LANES:]
    lower, upper = total[:slots], total[slots:]
    left = iota(lower.shape, 1) < HALF
    first_rows = jnp.where(left, lower, pltpu.roll(upper, HALF, 1))
    second_rows = jnp.where(left, pltpu.roll(lower, HALF, 1), upper)
    send_ref[...] = merge_pair(first_rows, second_rows)


def call(body, out_shape, *operands, scalars=0, scratch=()):
    vmem = pl.BlockSpec(memory_space=pltpu.VMEM)
    smem = pl.BlockSpec(memory_space=pltpu.SMEM)
    return pl.pallas_call(
        body,
        out_shape=out_shape,
        in_specs=[smem] * scalars + [vmem] * (len(operands) - scalars),
        out_specs=jax.tree.map(lambda _: vmem, out_shape),
        scratch_shapes=list(scratch),
        compiler_params=pltpu.CompilerParams(vmem_limit_bytes=VMEM_LIMIT),
    )(*operands)


def exchange(rows, peers):
    shape = (peers, rows.shape[0] // peers, LANES)
    return lax.all_to_all(rows.reshape(shape), GROUP, 0, 0, tiled=True).reshape(rows.shape)


def swap(values):
    side = lax.axis_size("sec")
    pairs = [(i * side + j, j * side + i) for i in range(side) for j in range(side)]
    return lax.ppermute(values, ("sec", "far"), pairs)


def shards(
    gas_field,
    parcel_state,
    parcel_mass,
    base_time,
    evap_rate,
    slot_blocks,
    parcel_block_slot,
    parcel_cell,
    parcel_count,
):
    along_x, pencils, along_z = gas_field.shape[1:]
    per_pencil = along_z // LANES
    blocks = along_x * pencils * per_pencil
    peers, per_peer = slot_blocks.shape[1:]
    slots = peers * per_peer
    lines = parcel_mass.shape[0] // LANES
    rows = 2 * slots

    def shape(dims, kind=F32):
        return jax.ShapeDtypeStruct(dims, kind)

    lists = swap(slot_blocks)
    own_gas = gas_field.reshape(along_x, pencils, per_pencil, LANES)
    own_gas = jnp.swapaxes(own_gas, 1, 2).reshape(blocks, LANES)
    own_drop = parcel_state.reshape(lines, LANES)
    together = lax.all_gather(
        jnp.concatenate([own_gas, own_drop], axis=0), "sec", axis=0, tiled=True
    )
    lists, together = lax.optimization_barrier((lists, together))
    wanted = call(
        functools.partial(order_kernel, per_peer, pencils, per_pencil, blocks),
        shape((rows, LANES), BF16),
        lists,
    )
    wanted = exchange(wanted, peers)
    pack = call(
        functools.partial(pack_kernel, slots),
        shape((2 * blocks + 7 * lines, LANES)),
        parcel_count,
        together,
        own_gas,
        own_drop,
        *(
            part.reshape(lines, LANES)
            for part in (parcel_mass, base_time, evap_rate, parcel_block_slot, parcel_cell)
        ),
        scalars=1,
    )
    pack = swap(pack)

    gas_shape = shape((2 * blocks, LANES))
    send_shape = shape((rows, LANES), BF16)
    pick, place, send = call(
        pick_kernel,
        (shape((rows, 2 * blocks), BF16), shape((2 * blocks, rows), BF16), send_shape),
        wanted,
        pack,
    )
    gas, state = pack, ()
    for substep in range(ITERS):
        last = substep == ITERS - 1
        recv = exchange(send, peers)
        state, source = call(
            functools.partial(parcel_kernel, 4, substep == 0),
            (shape((2 if last else 3, lines, LANES)), shape((rows, LANES))),
            recv,
            pack,
            *state,
            scratch=[pltpu.VMEM((2, lines, LANES), F32), pltpu.VMEM((4, lines, LANES), F32)],
        )
        source = exchange(source, peers)
        update = functools.partial(gas_kernel, pencils, per_pencil)
        if last:
            gas = call(update, shape((blocks, LANES)), source, gas, pick, place)
        else:
            gas, send = call(update, (gas_shape, send_shape), source, gas, pick, place)
            state = (state,)
    state = swap(state)
    gas = swap(gas).reshape(along_x, per_pencil, pencils, LANES)
    return (
        jnp.swapaxes(gas, 1, 2).reshape(gas_field.shape),
        state[OWN].reshape(parcel_state.shape),
        state[MASS].reshape(parcel_mass.shape),
    )


def solution(mesh):
    sec, row, col = (mesh.shape[name] for name in ("sec", "row", "col"))
    split = Mesh(mesh.devices.reshape(sec, row, sec, col // sec), ("sec", "row", "far", "near"))
    place = P(("row", "far", "near"))
    return jax.shard_map(
        shards,
        mesh=split,
        in_specs=(
            P("sec", "row", ("far", "near"), None),
            P("sec", ("row", "far", "near")),
            place,
            place,
            place,
            P(("row", "far", "near"), None, None),
            place,
            place,
            place,
        ),
        out_specs=(
            P("sec", "row", ("far", "near"), None),
            P("sec", ("row", "far", "near")),
            place,
        ),
        check_vma=False,
    )
```

```python
import functools

import jax
import jax.numpy as jnp
from jax import lax
from jax.experimental import pallas as pl
from jax.experimental.pallas import tpu as pltpu
from jax.sharding import Mesh
from jax.sharding import PartitionSpec as P

ITERS = 4
LATENT = 2.0
DEPOSIT_MODE = 0.5
ADVECT = 0.3
DIFFUSE = 0.2
LANES = 128
HALF = 64
GROUP = ("sec", "near")
OWN, MASS, TEMP, BASE, EVAP, SLOT, CELL = range(7)
VMEM_LIMIT = 32 * 1024 * 1024

F32 = jnp.float32
BF16 = jnp.bfloat16


def iota(shape, axis):
    return lax.broadcasted_iota(jnp.int32, shape, axis)


def dot(left_side, right_side, left_axis=1, right_axis=0):
    return lax.dot_general(
        left_side,
        right_side,
        (((left_axis,), (right_axis,)), ((), ())),
        preferred_element_type=F32,
    )


def thirds(values):
    high = values.astype(BF16).astype(F32)
    rest = values - high
    middle = rest.astype(BF16).astype(F32)
    return high, middle, rest - middle


def split_pair(rows):
    tiles = rows.reshape(rows.shape[0] // 16, 2, 8, LANES)
    even, odd = tiles[:, 0], tiles[:, 1]
    low = iota(even.shape, 1) < 4
    first = jnp.where(low, even, pltpu.roll(odd, 4, 1))
    second = jnp.where(low, pltpu.roll(even, 4, 1), odd)
    flat = (rows.shape[0] // 2, LANES)
    return first.reshape(flat), second.reshape(flat)


def merge_pair(first, second):
    shape = (first.shape[0] // 8, 8, LANES)
    first, second = first.reshape(shape), second.reshape(shape)
    low = iota(shape, 1) < 4
    even = jnp.where(low, first, pltpu.roll(second, 4, 1))
    odd = jnp.where(low, pltpu.roll(first, 4, 1), second)
    return jnp.stack([even, odd], axis=1).reshape(2 * shape[0] * 8, LANES)


def list_kernel(side, pencils, per_pencil, list_ref, out_ref):
    block = list_ref[0]
    first = block // (pencils * per_pencil)
    rest = block - first * (pencils * per_pencil)
    pencil = rest // per_pencil
    line = first * (pencils * per_pencil) + (rest - pencil * per_pencil) * pencils + pencil
    peers, per_peer = block.shape
    slots = peers * per_peer
    owner = (iota((slots, peers), 0) // per_peer == iota((slots, peers), 1)).astype(BF16)
    spread = dot(owner, line.astype(F32).astype(BF16))
    mine = iota(spread.shape, 0) % per_peer == iota(spread.shape, 1)
    value = jnp.sum(jnp.where(mine, spread, 0.0), axis=1, keepdims=True)
    value = jnp.broadcast_to(value, (slots, LANES))
    height = slots // side
    for i in range(side):
        for j in range(side):
            at = (i * side + j) * height
            out_ref[at : at + height] = value[i * height : (i + 1) * height]


def pack_kernel(
    slots, count_ref, temp_ref, gas_ref, drop_ref, mass_ref, base_ref, evap_ref, slot_ref, cell_ref, out_ref
):
    blocks, lines = gas_ref.shape[0], mass_ref.shape[0]
    start = temp_ref.shape[0] - blocks - lines
    out_ref[:blocks] = gas_ref[...]
    out_ref[blocks : 2 * blocks] = temp_ref[start : start + blocks]

    def store(which, values):
        at = 2 * blocks + which * lines
        out_ref[at : at + lines] = values

    store(OWN, drop_ref[...])
    store(MASS, mass_ref[...])
    store(TEMP, temp_ref[start + blocks :])
    store(BASE, base_ref[...])
    store(EVAP, evap_ref[...])
    shape = mass_ref.shape
    active = iota(shape, 0) * LANES + iota(shape, 1) < count_ref[0]
    upper = cell_ref[...] // HALF
    store(SLOT, (slot_ref[...] + slots * upper).astype(F32))
    store(CELL, jnp.where(active, cell_ref[...] - HALF * upper, -1).astype(F32))


def pick_kernel(list_ref, pack_ref, pick_ref, place_ref, send_ref):
    rows, columns = pick_ref.shape
    lines = list_ref[: rows // 2]
    wanted = merge_pair(lines, lines + columns / 2)
    pick = (wanted == iota((rows, columns), 1).astype(F32)).astype(F32)
    pick_ref[...] = pick.astype(BF16)
    place_ref[...] = pick.T.astype(BF16)
    gas = pack_ref[:columns]
    send_ref[...] = dot(pick.astype(BF16), gas.astype(BF16)).astype(BF16)


def gas_kernel(stride, per_pencil, source_ref, gas_ref, pick_ref, place_ref, gas_out, send_ref=None):
    place = place_ref[...]
    high, middle, low = (dot(place, part.astype(BF16)) for part in thirds(source_ref[...]))
    deposit = high + (middle + low)
    rows = place.shape[0]
    gas = gas_ref[:rows]
    block = iota(gas.shape, 0) // stride % per_pencil
    lane = iota(gas.shape, 1)
    to_right = pltpu.roll(gas, 1, 1)
    to_left = pltpu.roll(gas, LANES - 1, 1)
    left = jnp.where(
        lane == 0, jnp.where(block == 0, gas, pltpu.roll(to_right, stride, 0)), to_right
    )
    right = jnp.where(
        lane == LANES - 1,
        jnp.where(block == per_pencil - 1, gas, pltpu.roll(to_left, rows - stride, 0)),
        to_left,
    )
    moved = gas + ADVECT * (left - gas) + DIFFUSE * (right - 2.0 * gas + left)
    new_gas = moved + DEPOSIT_MODE * deposit
    gas_out[...] = new_gas[: gas_out.shape[0]]
    if send_ref is not None:
        send_ref[...] = dot(pick_ref[...], new_gas.astype(BF16)).astype(BF16)


def parcel_kernel(chunk, first, recv_ref, pack_ref, *refs):
    state_ref = None if first else refs[0]
    state_out, send_ref, seen_ref, part_ref = refs[-4:]
    lines = state_out.shape[1]
    base_row = pack_ref.shape[0] - 7 * lines
    slots = recv_ref.shape[0] // 2
    width = chunk * LANES

    def given(which):
        return pack_ref[base_row + which * lines : base_row + (which + 1) * lines]

    def held(which):
        return given(which) if first else state_ref[which]

    def fold(values):
        turned = values.T
        return jnp.concatenate([turned[:HALF], turned[HALF:]], axis=1)

    own, temp = split_pair(recv_ref[...].astype(F32))
    table = jnp.concatenate([fold(own), fold(temp)], axis=0).astype(BF16)

    def packed(ref, start):
        row = jnp.concatenate([ref[start + i : start + i + 1, :] for i in range(chunk)], axis=1)
        return jnp.broadcast_to(row, (16, width)).astype(BF16)[None]

    def index(count):
        shape = (count // 16, 16, width)
        return (iota(shape, 0) * 16 + iota(shape, 1)).astype(F32).astype(BF16)

    slot_index, cell_index = index(2 * slots), index(HALF)
    one, zero = jnp.ones((), BF16), jnp.zeros((), BF16)

    def masks(start):
        hot = jnp.where(slot_index == packed(pack_ref, base_row + SLOT * lines + start), one, zero)
        here = cell_index == packed(pack_ref, base_row + CELL * lines + start)
        return hot.reshape(2 * slots, width), here

    for start in range(0, lines, chunk):
        hot, here = masks(start)
        values = dot(table, hot).astype(BF16).reshape(2, HALF // 16, 16, width)
        for quantity in range(2):
            kept = jnp.where(here, values[quantity], zero)
            total = kept[0]
            for i in range(1, HALF // 16):
                total = total + kept[i]
            seen = jnp.sum(total.astype(F32), axis=0, keepdims=True)
            for i in range(chunk):
                seen_ref[quantity, start + i : start + i + 1, :] = seen[:, i * LANES : (i + 1) * LANES]

    hot_quantity = lax.axis_index("far") == 3
    own_heat = jnp.where(hot_quantity, 1.5, 1.0).astype(F32)
    own_latent = jnp.where(hot_quantity, LATENT, 0.0).astype(F32)
    active = given(CELL) >= 0.0
    mass = held(MASS)
    evap_now = given(EVAP) * jax.nn.sigmoid(seen_ref[1] - held(TEMP))
    new_mass = jnp.where(active, mass * jnp.exp(-evap_now), mass)
    state_out[MASS] = new_mass
    unit_time = given(BASE) * jnp.exp(jnp.log(mass) * (2.0 / 3.0))
    work = ((OWN, own_heat, own_latent), (TEMP, 1.5, LATENT))
    for quantity, (which, heat, latent) in enumerate(work):
        seen, drop = seen_ref[quantity], held(which)
        relaxed = seen + (drop - seen) * jnp.exp(-1.0 / (unit_time * heat))
        new_drop = jnp.where(active, relaxed, drop)
        if which < state_out.shape[0]:
            state_out[which] = new_drop
        source = mass * drop - new_mass * new_drop - latent * (mass - new_mass)
        for i, part in enumerate(thirds(source)):
            part_ref[2 * i + quantity] = part

    total = jnp.zeros((2 * slots, 6 * HALF), F32)
    for start in range(0, lines, chunk):
        hot, here = masks(start)
        parts = [
            jnp.where(here, packed(part_ref.at[i], start), zero).reshape(HALF, width)
            for i in range(6)
        ]
        total += dot(hot, jnp.concatenate(parts, axis=0), 1, 1)
    total = total[:, :LANES] + (total[:, LANES : 2 * LANES] + total[:, 2 * LANES :])
    lower, upper = total[:slots], total[slots:]
    left = iota(lower.shape, 1) < HALF
    first_rows = jnp.where(left, lower, pltpu.roll(upper, HALF, 1))
    second_rows = jnp.where(left, pltpu.roll(lower, HALF, 1), upper)
    send_ref[...] = merge_pair(first_rows, second_rows)


def call(body, out_shape, *operands, scalars=0, scratch=()):
    vmem = pl.BlockSpec(memory_space=pltpu.VMEM)
    smem = pl.BlockSpec(memory_space=pltpu.SMEM)
    return pl.pallas_call(
        body,
        out_shape=out_shape,
        in_specs=[smem] * scalars + [vmem] * (len(operands) - scalars),
        out_specs=jax.tree.map(lambda _: vmem, out_shape),
        scratch_shapes=list(scratch),
        compiler_params=pltpu.CompilerParams(vmem_limit_bytes=VMEM_LIMIT),
    )(*operands)


def exchange(rows, peers):
    shape = (peers, rows.shape[0] // peers, LANES)
    return lax.all_to_all(rows.reshape(shape), GROUP, 0, 0, tiled=True).reshape(rows.shape)


def swap(values):
    side = lax.axis_size("sec")
    pairs = [(i * side + j, j * side + i) for i in range(side) for j in range(side)]
    return lax.ppermute(values, ("sec", "far"), pairs)


def shards(
    gas_field,
    parcel_state,
    parcel_mass,
    base_time,
    evap_rate,
    slot_blocks,
    parcel_block_slot,
    parcel_cell,
    parcel_count,
):
    along_x, pencils, along_z = gas_field.shape[1:]
    per_pencil = along_z // LANES
    blocks = along_x * pencils * per_pencil
    peers, per_peer = slot_blocks.shape[1:]
    slots = peers * per_peer
    lines = parcel_mass.shape[0] // LANES
    rows = 2 * slots

    def shape(dims, kind=F32):
        return jax.ShapeDtypeStruct(dims, kind)

    side = lax.axis_size("sec")
    lists = call(
        functools.partial(list_kernel, side, pencils, per_pencil),
        shape((side * slots, LANES)),
        slot_blocks,
    ).reshape(side * peers, per_peer, LANES)
    lists = lax.all_to_all(lists, ("sec", "far", "near"), 0, 0, tiled=True)
    lists = lists.reshape(side * slots, LANES)
    own_gas = gas_field.reshape(along_x, pencils, per_pencil, LANES)
    own_gas = jnp.swapaxes(own_gas, 1, 2).reshape(blocks, LANES)
    own_drop = parcel_state.reshape(lines, LANES)
    together = lax.all_gather(
        jnp.concatenate([own_gas, own_drop], axis=0), "sec", axis=0, tiled=True
    )
    pack = call(
        functools.partial(pack_kernel, slots),
        shape((2 * blocks + 7 * lines, LANES)),
        parcel_count,
        together,
        own_gas,
        own_drop,
        *(
            part.reshape(lines, LANES)
            for part in (parcel_mass, base_time, evap_rate, parcel_block_slot, parcel_cell)
        ),
        scalars=1,
    )
    pack = swap(pack)

    gas_shape = shape((2 * blocks, LANES))
    send_shape = shape((rows, LANES), BF16)
    pick, place, send = call(
        pick_kernel,
        (shape((rows, 2 * blocks), BF16), shape((2 * blocks, rows), BF16), send_shape),
        lists,
        pack,
    )
    gas, state = pack, ()
    for substep in range(ITERS):
        last = substep == ITERS - 1
        recv = exchange(send, peers)
        state, source = call(
            functools.partial(parcel_kernel, 4, substep == 0),
            (shape((2 if last else 3, lines, LANES)), shape((rows, LANES))),
            recv,
            pack,
            *state,
            scratch=[pltpu.VMEM((2, lines, LANES), F32), pltpu.VMEM((6, lines, LANES), F32)],
        )
        source = exchange(source, peers)
        update = functools.partial(gas_kernel, pencils, per_pencil)
        if last:
            gas = call(update, shape((blocks, LANES)), source, gas, pick, place)
        else:
            gas, send = call(update, (gas_shape, send_shape), source, gas, pick, place)
            state = (state,)
    state = swap(state)
    gas = swap(gas).reshape(along_x, per_pencil, pencils, LANES)
    return (
        jnp.swapaxes(gas, 1, 2).reshape(gas_field.shape),
        state[OWN].reshape(parcel_state.shape),
        state[MASS].reshape(parcel_mass.shape),
    )


def solution(mesh):
    sec, row, col = (mesh.shape[name] for name in ("sec", "row", "col"))
    split = Mesh(mesh.devices.reshape(sec, row, sec, col // sec), ("sec", "row", "far", "near"))
    place = P(("row", "far", "near"))
    return jax.shard_map(
        shards,
        mesh=split,
        in_specs=(
            P("sec", "row", ("far", "near"), None),
            P("sec", ("row", "far", "near")),
            place,
            place,
            place,
            P(("row", "far", "near"), None, None),
            place,
            place,
            place,
        ),
        out_specs=(
            P("sec", "row", ("far", "near"), None),
            P("sec", ("row", "far", "near")),
            place,
        ),
        check_vma=False,
    )
```

```python
import functools

import jax
import jax.numpy as jnp
from jax import lax
from jax.experimental import pallas as pl
from jax.experimental.pallas import tpu as pltpu
from jax.sharding import Mesh
from jax.sharding import PartitionSpec as P

ITERS = 4
LATENT = 2.0
DEPOSIT_MODE = 0.5
ADVECT = 0.3
DIFFUSE = 0.2
LANES = 128
HALF = 64
GROUP = ("sec", "near")
OWN, MASS, TEMP, BASE, EVAP, SLOT, CELL = range(7)
VMEM_LIMIT = 32 * 1024 * 1024

F32 = jnp.float32
BF16 = jnp.bfloat16


def iota(shape, axis):
    return lax.broadcasted_iota(jnp.int32, shape, axis)


def dot(left_side, right_side, left_axis=1, right_axis=0):
    return lax.dot_general(
        left_side,
        right_side,
        (((left_axis,), (right_axis,)), ((), ())),
        preferred_element_type=F32,
    )


def thirds(values):
    high = values.astype(BF16).astype(F32)
    rest = values - high
    middle = rest.astype(BF16).astype(F32)
    return high, middle, rest - middle


def split_pair(rows):
    tiles = rows.reshape(rows.shape[0] // 16, 2, 8, LANES)
    even, odd = tiles[:, 0], tiles[:, 1]
    low = iota(even.shape, 1) < 4
    first = jnp.where(low, even, pltpu.roll(odd, 4, 1))
    second = jnp.where(low, pltpu.roll(even, 4, 1), odd)
    flat = (rows.shape[0] // 2, LANES)
    return first.reshape(flat), second.reshape(flat)


def merge_pair(first, second):
    shape = (first.shape[0] // 8, 8, LANES)
    first, second = first.reshape(shape), second.reshape(shape)
    low = iota(shape, 1) < 4
    even = jnp.where(low, first, pltpu.roll(second, 4, 1))
    odd = jnp.where(low, pltpu.roll(first, 4, 1), second)
    return jnp.stack([even, odd], axis=1).reshape(2 * shape[0] * 8, LANES)


def order_kernel(per_peer, pencils, per_pencil, blocks, list_ref, rows_ref):
    block = list_ref[0]
    first = block // (pencils * per_pencil)
    rest = block - first * (pencils * per_pencil)
    pencil = rest // per_pencil
    place = first * (pencils * per_pencil) + (rest - pencil * per_pencil) * pencils + pencil
    rows, peers = rows_ref.shape[0], block.shape[0]
    each = rows // peers
    owner = (iota((rows, peers), 0) // each == iota((rows, peers), 1)).astype(BF16)
    spread = dot(owner, place.astype(F32).astype(BF16))
    within = iota(spread.shape, 0) % each
    kept = jnp.where(within % per_peer == iota(spread.shape, 1), spread, 0.0)
    value = jnp.sum(kept, axis=1, keepdims=True)
    value = value + (blocks * (within[:, :1] // per_peer)).astype(F32)
    rows_ref[...] = jnp.broadcast_to(value, rows_ref.shape).astype(BF16)


def pack_kernel(
    slots, count_ref, temp_ref, gas_ref, drop_ref, mass_ref, base_ref, evap_ref, slot_ref, cell_ref, out_ref
):
    blocks, lines = gas_ref.shape[0], mass_ref.shape[0]
    start = temp_ref.shape[0] - blocks - lines
    out_ref[:blocks] = gas_ref[...]
    out_ref[blocks : 2 * blocks] = temp_ref[start : start + blocks]

    def store(which, values):
        at = 2 * blocks + which * lines
        out_ref[at : at + lines] = values

    store(OWN, drop_ref[...])
    store(MASS, mass_ref[...])
    store(TEMP, temp_ref[start + blocks :])
    store(BASE, base_ref[...])
    store(EVAP, evap_ref[...])
    shape = mass_ref.shape
    active = iota(shape, 0) * LANES + iota(shape, 1) < count_ref[0]
    upper = cell_ref[...] // HALF
    store(SLOT, (slot_ref[...] + slots * upper).astype(F32))
    store(CELL, jnp.where(active, cell_ref[...] - HALF * upper, -1).astype(F32))


def pick_kernel(wanted_ref, pack_ref, pick_ref, place_ref, send_ref):
    wanted = wanted_ref[...].astype(F32).astype(jnp.int32)
    pick = (wanted == iota(wanted.shape, 1)).astype(F32)
    pick_ref[...] = pick.astype(BF16)
    place_ref[...] = pick.T.astype(BF16)
    gas = pack_ref[: wanted.shape[1]]
    send_ref[...] = dot(pick.astype(BF16), gas.astype(BF16)).astype(BF16)


def gas_kernel(stride, per_pencil, source_ref, gas_ref, pick_ref, place_ref, gas_out, send_ref=None):
    place = place_ref[...]
    high, middle, low = (dot(place, part.astype(BF16)) for part in thirds(source_ref[...]))
    deposit = high + (middle + low)
    rows = place.shape[0]
    gas = gas_ref[:rows]
    block = iota(gas.shape, 0) // stride % per_pencil
    lane = iota(gas.shape, 1)
    to_right = pltpu.roll(gas, 1, 1)
    to_left = pltpu.roll(gas, LANES - 1, 1)
    left = jnp.where(
        lane == 0, jnp.where(block == 0, gas, pltpu.roll(to_right, stride, 0)), to_right
    )
    right = jnp.where(
        lane == LANES - 1,
        jnp.where(block == per_pencil - 1, gas, pltpu.roll(to_left, rows - stride, 0)),
        to_left,
    )
    moved = gas + ADVECT * (left - gas) + DIFFUSE * (right - 2.0 * gas + left)
    new_gas = moved + DEPOSIT_MODE * deposit
    gas_out[...] = new_gas[: gas_out.shape[0]]
    if send_ref is not None:
        send_ref[...] = dot(pick_ref[...], new_gas.astype(BF16)).astype(BF16)


def parcel_kernel(chunk, first, recv_ref, pack_ref, *refs):
    state_ref = None if first else refs[0]
    state_out, send_ref, seen_ref, part_ref = refs[-4:]
    lines = state_out.shape[1]
    base_row = pack_ref.shape[0] - 7 * lines
    slots = recv_ref.shape[0] // 2
    width = chunk * LANES

    def given(which):
        return pack_ref[base_row + which * lines : base_row + (which + 1) * lines]

    def held(which):
        return given(which) if first else state_ref[which]

    def fold(values):
        turned = values.T
        return jnp.concatenate([turned[:HALF], turned[HALF:]], axis=1)

    own, temp = split_pair(recv_ref[...].astype(F32))
    table = jnp.concatenate([fold(own), fold(temp)], axis=0).astype(BF16)

    def packed(ref, start):
        row = jnp.concatenate([ref[start + i : start + i + 1, :] for i in range(chunk)], axis=1)
        return jnp.broadcast_to(row, (16, width)).astype(BF16)[None]

    def index(count):
        shape = (count // 16, 16, width)
        return (iota(shape, 0) * 16 + iota(shape, 1)).astype(F32).astype(BF16)

    slot_index, cell_index = index(2 * slots), index(HALF)
    one, zero = jnp.ones((), BF16), jnp.zeros((), BF16)

    def masks(start):
        hot = jnp.where(slot_index == packed(pack_ref, base_row + SLOT * lines + start), one, zero)
        here = cell_index == packed(pack_ref, base_row + CELL * lines + start)
        return hot.reshape(2 * slots, width), here

    for start in range(0, lines, chunk):
        hot, here = masks(start)
        values = dot(table, hot).astype(BF16).reshape(2, HALF // 16, 16, width)
        for quantity in range(2):
            kept = jnp.where(here, values[quantity], zero)
            total = kept[0]
            for i in range(1, HALF // 16):
                total = total + kept[i]
            seen = jnp.sum(total.astype(F32), axis=0, keepdims=True)
            for i in range(chunk):
                seen_ref[quantity, start + i : start + i + 1, :] = seen[:, i * LANES : (i + 1) * LANES]

    hot_quantity = lax.axis_index("far") == 3
    own_heat = jnp.where(hot_quantity, 1.5, 1.0).astype(F32)
    own_latent = jnp.where(hot_quantity, LATENT, 0.0).astype(F32)
    active = given(CELL) >= 0.0
    mass = held(MASS)
    evap_now = given(EVAP) * jax.nn.sigmoid(seen_ref[1] - held(TEMP))
    new_mass = jnp.where(active, mass * jnp.exp(-evap_now), mass)
    state_out[MASS] = new_mass
    unit_time = given(BASE) * jnp.exp(jnp.log(mass) * (2.0 / 3.0))
    work = ((OWN, own_heat, own_latent), (TEMP, 1.5, LATENT))
    for quantity, (which, heat, latent) in enumerate(work):
        seen, drop = seen_ref[quantity], held(which)
        relaxed = seen + (drop - seen) * jnp.exp(-1.0 / (unit_time * heat))
        new_drop = jnp.where(active, relaxed, drop)
        if which < state_out.shape[0]:
            state_out[which] = new_drop
        source = mass * drop - new_mass * new_drop - latent * (mass - new_mass)
        for i, part in enumerate(thirds(source)):
            part_ref[2 * i + quantity] = part

    total = jnp.zeros((2 * slots, 6 * HALF), F32)
    for start in range(0, lines, chunk):
        hot, here = masks(start)
        parts = [
            jnp.where(here, packed(part_ref.at[i], start), zero).reshape(HALF, width)
            for i in range(6)
        ]
        total += dot(hot, jnp.concatenate(parts, axis=0), 1, 1)
    total = total[:, :LANES] + (total[:, LANES : 2 * LANES] + total[:, 2 * LANES :])
    lower, upper = total[:slots], total[slots:]
    left = iota(lower.shape, 1) < HALF
    first_rows = jnp.where(left, lower, pltpu.roll(upper, HALF, 1))
    second_rows = jnp.where(left, pltpu.roll(lower, HALF, 1), upper)
    send_ref[...] = merge_pair(first_rows, second_rows)


def call(body, out_shape, *operands, scalars=0, scratch=()):
    vmem = pl.BlockSpec(memory_space=pltpu.VMEM)
    smem = pl.BlockSpec(memory_space=pltpu.SMEM)
    return pl.pallas_call(
        body,
        out_shape=out_shape,
        in_specs=[smem] * scalars + [vmem] * (len(operands) - scalars),
        out_specs=jax.tree.map(lambda _: vmem, out_shape),
        scratch_shapes=list(scratch),
        compiler_params=pltpu.CompilerParams(vmem_limit_bytes=VMEM_LIMIT),
    )(*operands)


def exchange(rows, peers):
    shape = (peers, rows.shape[0] // peers, LANES)
    return lax.all_to_all(rows.reshape(shape), GROUP, 0, 0, tiled=True).reshape(rows.shape)


def swap(values):
    side = lax.axis_size("sec")
    pairs = [(i * side + j, j * side + i) for i in range(side) for j in range(side)]
    return lax.ppermute(values, ("sec", "far"), pairs)


def shards(
    gas_field,
    parcel_state,
    parcel_mass,
    base_time,
    evap_rate,
    slot_blocks,
    parcel_block_slot,
    parcel_cell,
    parcel_count,
):
    along_x, pencils, along_z = gas_field.shape[1:]
    per_pencil = along_z // LANES
    blocks = along_x * pencils * per_pencil
    peers, per_peer = slot_blocks.shape[1:]
    slots = peers * per_peer
    lines = parcel_mass.shape[0] // LANES
    rows = 2 * slots

    def shape(dims, kind=F32):
        return jax.ShapeDtypeStruct(dims, kind)

    lists = swap(slot_blocks)
    own_gas = gas_field.reshape(along_x, pencils, per_pencil, LANES)
    own_gas = jnp.swapaxes(own_gas, 1, 2).reshape(blocks, LANES)
    own_drop = parcel_state.reshape(lines, LANES)
    together = lax.all_gather(
        jnp.concatenate([own_gas, own_drop], axis=0), "sec", axis=0, tiled=True
    )
    lists, together = lax.optimization_barrier((lists, together))
    wanted = call(
        functools.partial(order_kernel, per_peer, pencils, per_pencil, blocks),
        shape((rows, LANES), BF16),
        lists,
    )
    wanted = exchange(wanted, peers)
    pack = call(
        functools.partial(pack_kernel, slots),
        shape((2 * blocks + 7 * lines, LANES)),
        parcel_count,
        together,
        own_gas,
        own_drop,
        *(
            part.reshape(lines, LANES)
            for part in (parcel_mass, base_time, evap_rate, parcel_block_slot, parcel_cell)
        ),
        scalars=1,
    )
    pack = swap(pack)

    gas_shape = shape((2 * blocks, LANES))
    send_shape = shape((rows, LANES), BF16)
    pick, place, send = call(
        pick_kernel,
        (shape((rows, 2 * blocks), BF16), shape((2 * blocks, rows), BF16), send_shape),
        wanted,
        pack,
    )
    gas, state = pack, ()
    for substep in range(ITERS):
        last = substep == ITERS - 1
        recv = exchange(send, peers)
        state, source = call(
            functools.partial(parcel_kernel, 4, substep == 0),
            (shape((2 if last else 3, lines, LANES)), shape((rows, LANES))),
            recv,
            pack,
            *state,
            scratch=[pltpu.VMEM((2, lines, LANES), F32), pltpu.VMEM((6, lines, LANES), F32)],
        )
        source = exchange(source, peers)
        update = functools.partial(gas_kernel, pencils, per_pencil)
        if last:
            gas = call(update, shape((blocks, LANES)), source, gas, pick, place)
        else:
            gas, send = call(update, (gas_shape, send_shape), source, gas, pick, place)
            state = (state,)
    state = swap(state)
    gas = swap(gas).reshape(along_x, per_pencil, pencils, LANES)
    return (
        jnp.swapaxes(gas, 1, 2).reshape(gas_field.shape),
        state[OWN].reshape(parcel_state.shape),
        state[MASS].reshape(parcel_mass.shape),
    )


def solution(mesh):
    sec, row, col = (mesh.shape[name] for name in ("sec", "row", "col"))
    split = Mesh(mesh.devices.reshape(sec, row, sec, col // sec), ("sec", "row", "far", "near"))
    place = P(("row", "far", "near"))
    return jax.shard_map(
        shards,
        mesh=split,
        in_specs=(
            P("sec", "row", ("far", "near"), None),
            P("sec", ("row", "far", "near")),
            place,
            place,
            place,
            P(("row", "far", "near"), None, None),
            place,
            place,
            place,
        ),
        out_specs=(
            P("sec", "row", ("far", "near"), None),
            P("sec", ("row", "far", "near")),
            place,
        ),
        check_vma=False,
    )
```

```python
import functools

import jax
import jax.numpy as jnp
from jax import lax
from jax.experimental import pallas as pl
from jax.experimental.pallas import tpu as pltpu
from jax.sharding import Mesh
from jax.sharding import PartitionSpec as P

ITERS = 4
LATENT = 2.0
DEPOSIT_MODE = 0.5
ADVECT = 0.3
DIFFUSE = 0.2
LANES = 128
HALF = 64
GROUP = ("sec", "near")
OWN, MASS, TEMP, BASE, EVAP, SLOT, CELL = range(7)
VMEM_LIMIT = 32 * 1024 * 1024

F32 = jnp.float32
BF16 = jnp.bfloat16


def iota(shape, axis):
    return lax.broadcasted_iota(jnp.int32, shape, axis)


def dot(left_side, right_side, left_axis=1, right_axis=0):
    return lax.dot_general(
        left_side,
        right_side,
        (((left_axis,), (right_axis,)), ((), ())),
        preferred_element_type=F32,
    )


def thirds(values):
    high = values.astype(BF16).astype(F32)
    rest = values - high
    middle = rest.astype(BF16).astype(F32)
    return high, middle, rest - middle


def split_pair(rows):
    tiles = rows.reshape(rows.shape[0] // 16, 2, 8, LANES)
    even, odd = tiles[:, 0], tiles[:, 1]
    low = iota(even.shape, 1) < 4
    first = jnp.where(low, even, pltpu.roll(odd, 4, 1))
    second = jnp.where(low, pltpu.roll(even, 4, 1), odd)
    flat = (rows.shape[0] // 2, LANES)
    return first.reshape(flat), second.reshape(flat)


def merge_pair(first, second):
    shape = (first.shape[0] // 8, 8, LANES)
    first, second = first.reshape(shape), second.reshape(shape)
    low = iota(shape, 1) < 4
    even = jnp.where(low, first, pltpu.roll(second, 4, 1))
    odd = jnp.where(low, pltpu.roll(first, 4, 1), second)
    return jnp.stack([even, odd], axis=1).reshape(2 * shape[0] * 8, LANES)


def order_kernel(per_peer, pencils, per_pencil, blocks, list_ref, rows_ref):
    block = list_ref[0]
    first = block // (pencils * per_pencil)
    rest = block - first * (pencils * per_pencil)
    pencil = rest // per_pencil
    place = first * (pencils * per_pencil) + (rest - pencil * per_pencil) * pencils + pencil
    rows, peers = rows_ref.shape[0], block.shape[0]
    each = rows // peers
    owner = (iota((rows, peers), 0) // each == iota((rows, peers), 1)).astype(BF16)
    spread = dot(owner, place.astype(F32).astype(BF16))
    within = iota(spread.shape, 0) % each
    kept = jnp.where(within % per_peer == iota(spread.shape, 1), spread, 0.0)
    value = jnp.sum(kept, axis=1, keepdims=True)
    value = value + (blocks * (within[:, :1] // per_peer)).astype(F32)
    rows_ref[...] = jnp.broadcast_to(value, rows_ref.shape).astype(BF16)


def pack_kernel(
    slots, count_ref, temp_ref, gas_ref, drop_ref, mass_ref, base_ref, evap_ref, slot_ref, cell_ref, out_ref
):
    blocks, lines = gas_ref.shape[0], mass_ref.shape[0]
    start = temp_ref.shape[0] - blocks - lines
    out_ref[:blocks] = gas_ref[...]
    out_ref[blocks : 2 * blocks] = temp_ref[start : start + blocks]

    def store(which, values):
        at = 2 * blocks + which * lines
        out_ref[at : at + lines] = values

    store(OWN, drop_ref[...])
    store(MASS, mass_ref[...])
    store(TEMP, temp_ref[start + blocks :])
    store(BASE, base_ref[...])
    store(EVAP, evap_ref[...])
    shape = mass_ref.shape
    active = iota(shape, 0) * LANES + iota(shape, 1) < count_ref[0]
    upper = cell_ref[...] // HALF
    store(SLOT, (slot_ref[...] + slots * upper).astype(F32))
    store(CELL, jnp.where(active, cell_ref[...] - HALF * upper, -1).astype(F32))


def pick_kernel(wanted_ref, pack_ref, pick_ref, place_ref, own_place_ref, send_ref):
    wanted = wanted_ref[...].astype(F32)
    own = split_pair(wanted)[0]
    own = (own == iota(own.shape, 1).astype(F32)).astype(F32)
    own_place_ref[...] = own.T[: own_place_ref.shape[0]].astype(BF16)
    wanted = wanted.astype(jnp.int32)
    pick = (wanted == iota(wanted.shape, 1)).astype(F32)
    pick_ref[...] = pick.astype(BF16)
    place_ref[...] = pick.T.astype(BF16)
    gas = pack_ref[: wanted.shape[1]]
    send_ref[...] = dot(pick.astype(BF16), gas.astype(BF16)).astype(BF16)


def gas_kernel(stride, per_pencil, source_ref, gas_ref, pick_ref, place_ref, gas_out, send_ref=None):
    place = place_ref[...]
    high, middle, low = (dot(place, part.astype(BF16)) for part in thirds(source_ref[...]))
    deposit = high + (middle + low)
    rows = place.shape[0]
    gas = gas_ref[:rows]
    block = iota(gas.shape, 0) // stride % per_pencil
    lane = iota(gas.shape, 1)
    to_right = pltpu.roll(gas, 1, 1)
    to_left = pltpu.roll(gas, LANES - 1, 1)
    left = jnp.where(
        lane == 0, jnp.where(block == 0, gas, pltpu.roll(to_right, stride, 0)), to_right
    )
    right = jnp.where(
        lane == LANES - 1,
        jnp.where(block == per_pencil - 1, gas, pltpu.roll(to_left, rows - stride, 0)),
        to_left,
    )
    moved = gas + ADVECT * (left - gas) + DIFFUSE * (right - 2.0 * gas + left)
    new_gas = moved + DEPOSIT_MODE * deposit
    gas_out[...] = new_gas[: gas_out.shape[0]]
    if send_ref is not None:
        send_ref[...] = dot(pick_ref[...], new_gas.astype(BF16)).astype(BF16)


def parcel_kernel(chunk, first, recv_ref, pack_ref, *refs):
    state_ref = None if first else refs[0]
    state_out, send_ref, seen_ref, part_ref = refs[-4:]
    lines = state_out.shape[1]
    base_row = pack_ref.shape[0] - 7 * lines
    slots = recv_ref.shape[0] // 2
    width = chunk * LANES

    def given(which):
        return pack_ref[base_row + which * lines : base_row + (which + 1) * lines]

    def held(which):
        return given(which) if first else state_ref[which]

    def fold(values):
        turned = values.T
        return jnp.concatenate([turned[:HALF], turned[HALF:]], axis=1)

    own, temp = split_pair(recv_ref[...].astype(F32))
    table = jnp.concatenate([fold(own), fold(temp)], axis=0).astype(BF16)

    def packed(ref, start):
        row = jnp.concatenate([ref[start + i : start + i + 1, :] for i in range(chunk)], axis=1)
        return jnp.broadcast_to(row, (16, width)).astype(BF16)[None]

    def index(count):
        shape = (count // 16, 16, width)
        return (iota(shape, 0) * 16 + iota(shape, 1)).astype(F32).astype(BF16)

    slot_index, cell_index = index(2 * slots), index(HALF)
    one, zero = jnp.ones((), BF16), jnp.zeros((), BF16)

    def masks(start):
        hot = jnp.where(slot_index == packed(pack_ref, base_row + SLOT * lines + start), one, zero)
        here = cell_index == packed(pack_ref, base_row + CELL * lines + start)
        return hot.reshape(2 * slots, width), here

    for start in range(0, lines, chunk):
        hot, here = masks(start)
        values = dot(table, hot).astype(BF16).reshape(2, HALF // 16, 16, width)
        for quantity in range(2):
            kept = jnp.where(here, values[quantity], zero)
            total = kept[0]
            for i in range(1, HALF // 16):
                total = total + kept[i]
            seen = jnp.sum(total.astype(F32), axis=0, keepdims=True)
            for i in range(chunk):
                seen_ref[quantity, start + i : start + i + 1, :] = seen[:, i * LANES : (i + 1) * LANES]

    hot_quantity = lax.axis_index("far") == 3
    own_heat = jnp.where(hot_quantity, 1.5, 1.0).astype(F32)
    own_latent = jnp.where(hot_quantity, LATENT, 0.0).astype(F32)
    active = given(CELL) >= 0.0
    mass = held(MASS)
    evap_now = given(EVAP) * jax.nn.sigmoid(seen_ref[1] - held(TEMP))
    new_mass = jnp.where(active, mass * jnp.exp(-evap_now), mass)
    state_out[MASS] = new_mass
    unit_time = given(BASE) * jnp.exp(jnp.log(mass) * (2.0 / 3.0))
    work = ((OWN, own_heat, own_latent), (TEMP, 1.5, LATENT))
    for quantity, (which, heat, latent) in enumerate(work):
        seen, drop = seen_ref[quantity], held(which)
        relaxed = seen + (drop - seen) * jnp.exp(-1.0 / (unit_time * heat))
        new_drop = jnp.where(active, relaxed, drop)
        if which < state_out.shape[0]:
            state_out[which] = new_drop
        source = mass * drop - new_mass * new_drop - latent * (mass - new_mass)
        for i, part in enumerate(thirds(source)):
            part_ref[2 * i + quantity] = part

    sent = 2 if state_out.shape[0] > TEMP else 1
    total = jnp.zeros((3 * sent * HALF, 2 * slots), F32)
    for start in range(0, lines, chunk):
        hot, here = masks(start)
        parts = [
            jnp.where(here, packed(part_ref.at[2 * i + quantity], start), zero).reshape(HALF, width)
            for i in range(3)
            for quantity in range(sent)
        ]
        total += dot(jnp.concatenate(parts, axis=0), hot, 1, 1)
    high, middle, low = (total[i * sent * HALF : (i + 1) * sent * HALF] for i in range(3))
    total = high + (middle + low)

    def unfold(values):
        return jnp.concatenate([values[:, :slots], values[:, slots:]], axis=0).T

    own = unfold(total[:HALF])
    send_ref[...] = own if sent == 1 else merge_pair(own, unfold(total[HALF:]))


def call(body, out_shape, *operands, scalars=0, scratch=()):
    vmem = pl.BlockSpec(memory_space=pltpu.VMEM)
    smem = pl.BlockSpec(memory_space=pltpu.SMEM)
    return pl.pallas_call(
        body,
        out_shape=out_shape,
        in_specs=[smem] * scalars + [vmem] * (len(operands) - scalars),
        out_specs=jax.tree.map(lambda _: vmem, out_shape),
        scratch_shapes=list(scratch),
        compiler_params=pltpu.CompilerParams(vmem_limit_bytes=VMEM_LIMIT),
    )(*operands)


def exchange(rows, peers):
    shape = (peers, rows.shape[0] // peers, LANES)
    return lax.all_to_all(rows.reshape(shape), GROUP, 0, 0, tiled=True).reshape(rows.shape)


def swap(values):
    side = lax.axis_size("sec")
    pairs = [(i * side + j, j * side + i) for i in range(side) for j in range(side)]
    return lax.ppermute(values, ("sec", "far"), pairs)


def shards(
    gas_field,
    parcel_state,
    parcel_mass,
    base_time,
    evap_rate,
    slot_blocks,
    parcel_block_slot,
    parcel_cell,
    parcel_count,
):
    along_x, pencils, along_z = gas_field.shape[1:]
    per_pencil = along_z // LANES
    blocks = along_x * pencils * per_pencil
    peers, per_peer = slot_blocks.shape[1:]
    slots = peers * per_peer
    lines = parcel_mass.shape[0] // LANES
    rows = 2 * slots

    def shape(dims, kind=F32):
        return jax.ShapeDtypeStruct(dims, kind)

    lists = swap(slot_blocks)
    own_gas = gas_field.reshape(along_x, pencils, per_pencil, LANES)
    own_gas = jnp.swapaxes(own_gas, 1, 2).reshape(blocks, LANES)
    own_drop = parcel_state.reshape(lines, LANES)
    together = lax.all_gather(
        jnp.concatenate([own_gas, own_drop], axis=0), "sec", axis=0, tiled=True
    )
    lists, together = lax.optimization_barrier((lists, together))
    wanted = call(
        functools.partial(order_kernel, per_peer, pencils, per_pencil, blocks),
        shape((rows, LANES), BF16),
        lists,
    )
    wanted = exchange(wanted, peers)
    pack = call(
        functools.partial(pack_kernel, slots),
        shape((2 * blocks + 7 * lines, LANES)),
        parcel_count,
        together,
        own_gas,
        own_drop,
        *(
            part.reshape(lines, LANES)
            for part in (parcel_mass, base_time, evap_rate, parcel_block_slot, parcel_cell)
        ),
        scalars=1,
    )
    pack = swap(pack)

    gas_shape = shape((2 * blocks, LANES))
    send_shape = shape((rows, LANES), BF16)
    pick, place, own_place, send = call(
        pick_kernel,
        (
            shape((rows, 2 * blocks), BF16),
            shape((2 * blocks, rows), BF16),
            shape((blocks, slots), BF16),
            send_shape,
        ),
        wanted,
        pack,
    )
    gas, state = pack, ()
    for substep in range(ITERS):
        last = substep == ITERS - 1
        recv = exchange(send, peers)
        state, source = call(
            functools.partial(parcel_kernel, 4, substep == 0),
            (
                shape((2 if last else 3, lines, LANES)),
                shape((slots if last else rows, LANES)),
            ),
            recv,
            pack,
            *state,
            scratch=[pltpu.VMEM((2, lines, LANES), F32), pltpu.VMEM((6, lines, LANES), F32)],
        )
        source = exchange(source, peers)
        update = functools.partial(gas_kernel, pencils, per_pencil)
        if last:
            gas = call(update, shape((blocks, LANES)), source, gas, pick, own_place)
        else:
            gas, send = call(update, (gas_shape, send_shape), source, gas, pick, place)
            state = (state,)
    state = swap(state)
    gas = swap(gas).reshape(along_x, per_pencil, pencils, LANES)
    return (
        jnp.swapaxes(gas, 1, 2).reshape(gas_field.shape),
        state[OWN].reshape(parcel_state.shape),
        state[MASS].reshape(parcel_mass.shape),
    )


def solution(mesh):
    sec, row, col = (mesh.shape[name] for name in ("sec", "row", "col"))
    split = Mesh(mesh.devices.reshape(sec, row, sec, col // sec), ("sec", "row", "far", "near"))
    place = P(("row", "far", "near"))
    return jax.shard_map(
        shards,
        mesh=split,
        in_specs=(
            P("sec", "row", ("far", "near"), None),
            P("sec", ("row", "far", "near")),
            place,
            place,
            place,
            P(("row", "far", "near"), None, None),
            place,
            place,
            place,
        ),
        out_specs=(
            P("sec", "row", ("far", "near"), None),
            P("sec", ("row", "far", "near")),
            place,
        ),
        check_vma=False,
    )
```

```python
import functools

import jax
import jax.numpy as jnp
from jax import lax
from jax.experimental import pallas as pl
from jax.experimental.pallas import tpu as pltpu
from jax.sharding import Mesh
from jax.sharding import PartitionSpec as P

ITERS = 4
LATENT = 2.0
DEPOSIT_MODE = 0.5
ADVECT = 0.3
DIFFUSE = 0.2
LANES = 128
HALF = 64
GROUP = ("sec", "near")
OWN, MASS, TEMP, BASE, EVAP, SLOT, CELL = range(7)
VMEM_LIMIT = 32 * 1024 * 1024

F32 = jnp.float32
BF16 = jnp.bfloat16


def iota(shape, axis):
    return lax.broadcasted_iota(jnp.int32, shape, axis)


def dot(left_side, right_side, left_axis=1, right_axis=0):
    return lax.dot_general(
        left_side,
        right_side,
        (((left_axis,), (right_axis,)), ((), ())),
        preferred_element_type=F32,
    )


def thirds(values):
    high = values.astype(BF16).astype(F32)
    rest = values - high
    middle = rest.astype(BF16).astype(F32)
    return high, middle, rest - middle


def split_pair(rows):
    tiles = rows.reshape(rows.shape[0] // 16, 2, 8, LANES)
    even, odd = tiles[:, 0], tiles[:, 1]
    low = iota(even.shape, 1) < 4
    first = jnp.where(low, even, pltpu.roll(odd, 4, 1))
    second = jnp.where(low, pltpu.roll(even, 4, 1), odd)
    flat = (rows.shape[0] // 2, LANES)
    return first.reshape(flat), second.reshape(flat)


def merge_pair(first, second):
    shape = (first.shape[0] // 8, 8, LANES)
    first, second = first.reshape(shape), second.reshape(shape)
    low = iota(shape, 1) < 4
    even = jnp.where(low, first, pltpu.roll(second, 4, 1))
    odd = jnp.where(low, pltpu.roll(first, 4, 1), second)
    return jnp.stack([even, odd], axis=1).reshape(2 * shape[0] * 8, LANES)


def order_kernel(pencils, per_pencil, list_ref, rows_ref):
    block = list_ref[0]
    peers, per_peer = block.shape
    first = block // (pencils * per_pencil)
    rest = block - first * (pencils * per_pencil)
    pencil = rest // per_pencil
    line = first * (pencils * per_pencil) + (rest - pencil * per_pencil) * pencils + pencil
    slots = rows_ref.shape[0]
    owner = (iota((slots, peers), 0) // per_peer == iota((slots, peers), 1)).astype(BF16)
    spread = dot(owner, line.astype(F32).astype(BF16))
    mine = iota(spread.shape, 0) % per_peer == iota(spread.shape, 1)
    value = jnp.sum(jnp.where(mine, spread, 0.0), axis=1, keepdims=True)
    rows_ref[...] = jnp.broadcast_to(value, rows_ref.shape).astype(BF16)


def pack_kernel(
    slots, count_ref, temp_ref, gas_ref, drop_ref, mass_ref, base_ref, evap_ref, slot_ref, cell_ref, out_ref
):
    blocks, lines = gas_ref.shape[0], mass_ref.shape[0]
    start = temp_ref.shape[0] - blocks - lines
    out_ref[:blocks] = gas_ref[...]
    out_ref[blocks : 2 * blocks] = temp_ref[start : start + blocks]

    def store(which, values):
        at = 2 * blocks + which * lines
        out_ref[at : at + lines] = values

    store(OWN, drop_ref[...])
    store(MASS, mass_ref[...])
    store(TEMP, temp_ref[start + blocks :])
    store(BASE, base_ref[...])
    store(EVAP, evap_ref[...])
    shape = mass_ref.shape
    active = iota(shape, 0) * LANES + iota(shape, 1) < count_ref[0]
    upper = cell_ref[...] // HALF
    store(SLOT, (slot_ref[...] + slots * upper).astype(F32))
    store(CELL, jnp.where(active, cell_ref[...] - HALF * upper, -1).astype(F32))


def pick_kernel(wanted_ref, pack_ref, pick_ref, place_ref, own_place_ref, send_ref):
    lines = wanted_ref[...].astype(F32)
    own = (lines == iota(lines.shape, 1).astype(F32)).astype(F32)
    own_place_ref[...] = own.T[: own_place_ref.shape[0]].astype(BF16)
    wanted = merge_pair(lines, lines + pick_ref.shape[1] / 2)
    pick = (wanted == iota(pick_ref.shape, 1).astype(F32)).astype(F32)
    pick_ref[...] = pick.astype(BF16)
    place_ref[...] = pick.T.astype(BF16)
    gas = pack_ref[: pick_ref.shape[1]]
    send_ref[...] = dot(pick.astype(BF16), gas.astype(BF16)).astype(BF16)


def gas_kernel(stride, per_pencil, source_ref, gas_ref, pick_ref, place_ref, gas_out, send_ref=None):
    place = place_ref[...]
    high, middle, low = (dot(place, part.astype(BF16)) for part in thirds(source_ref[...]))
    deposit = high + (middle + low)
    rows = place.shape[0]
    gas = gas_ref[:rows]
    block = iota(gas.shape, 0) // stride % per_pencil
    lane = iota(gas.shape, 1)
    to_right = pltpu.roll(gas, 1, 1)
    to_left = pltpu.roll(gas, LANES - 1, 1)
    left = jnp.where(
        lane == 0, jnp.where(block == 0, gas, pltpu.roll(to_right, stride, 0)), to_right
    )
    right = jnp.where(
        lane == LANES - 1,
        jnp.where(block == per_pencil - 1, gas, pltpu.roll(to_left, rows - stride, 0)),
        to_left,
    )
    moved = gas + ADVECT * (left - gas) + DIFFUSE * (right - 2.0 * gas + left)
    new_gas = moved + DEPOSIT_MODE * deposit
    gas_out[...] = new_gas[: gas_out.shape[0]]
    if send_ref is not None:
        send_ref[...] = dot(pick_ref[...], new_gas.astype(BF16)).astype(BF16)


def parcel_kernel(chunk, first, recv_ref, pack_ref, *refs):
    state_ref = None if first else refs[0]
    state_out, send_ref, seen_ref, part_ref = refs[-4:]
    lines = state_out.shape[1]
    base_row = pack_ref.shape[0] - 7 * lines
    slots = recv_ref.shape[0] // 2
    width = chunk * LANES

    def given(which):
        return pack_ref[base_row + which * lines : base_row + (which + 1) * lines]

    def held(which):
        return given(which) if first else state_ref[which]

    def fold(values):
        turned = values.T
        return jnp.concatenate([turned[:HALF], turned[HALF:]], axis=1)

    own, temp = split_pair(recv_ref[...].astype(F32))
    table = jnp.concatenate([fold(own), fold(temp)], axis=0).astype(BF16)

    def packed(ref, start):
        row = jnp.concatenate([ref[start + i : start + i + 1, :] for i in range(chunk)], axis=1)
        return jnp.broadcast_to(row, (16, width)).astype(BF16)[None]

    def index(count):
        shape = (count // 16, 16, width)
        return (iota(shape, 0) * 16 + iota(shape, 1)).astype(F32).astype(BF16)

    slot_index, cell_index = index(2 * slots), index(HALF)
    one, zero = jnp.ones((), BF16), jnp.zeros((), BF16)

    def masks(start):
        hot = jnp.where(slot_index == packed(pack_ref, base_row + SLOT * lines + start), one, zero)
        here = cell_index == packed(pack_ref, base_row + CELL * lines + start)
        return hot.reshape(2 * slots, width), here

    for start in range(0, lines, chunk):
        hot, here = masks(start)
        values = dot(table, hot).astype(BF16).reshape(2, HALF // 16, 16, width)
        for quantity in range(2):
            kept = jnp.where(here, values[quantity], zero)
            total = kept[0]
            for i in range(1, HALF // 16):
                total = total + kept[i]
            seen = jnp.sum(total.astype(F32), axis=0, keepdims=True)
            for i in range(chunk):
                seen_ref[quantity, start + i : start + i + 1, :] = seen[:, i * LANES : (i + 1) * LANES]

    hot_quantity = lax.axis_index("far") == 3
    own_heat = jnp.where(hot_quantity, 1.5, 1.0).astype(F32)
    own_latent = jnp.where(hot_quantity, LATENT, 0.0).astype(F32)
    active = given(CELL) >= 0.0
    mass = held(MASS)
    evap_now = given(EVAP) * jax.nn.sigmoid(seen_ref[1] - held(TEMP))
    new_mass = jnp.where(active, mass * jnp.exp(-evap_now), mass)
    state_out[MASS] = new_mass
    unit_time = given(BASE) * jnp.exp(jnp.log(mass) * (2.0 / 3.0))
    work = ((OWN, own_heat, own_latent), (TEMP, 1.5, LATENT))
    for quantity, (which, heat, latent) in enumerate(work):
        seen, drop = seen_ref[quantity], held(which)
        relaxed = seen + (drop - seen) * jnp.exp(-1.0 / (unit_time * heat))
        new_drop = jnp.where(active, relaxed, drop)
        if which < state_out.shape[0]:
            state_out[which] = new_drop
        source = mass * drop - new_mass * new_drop - latent * (mass - new_mass)
        for i, part in enumerate(thirds(source)):
            part_ref[2 * i + quantity] = part

    sent = 2 if state_out.shape[0] > TEMP else 1
    total = jnp.zeros((3 * sent * HALF, 2 * slots), F32)
    for start in range(0, lines, chunk):
        hot, here = masks(start)
        parts = [
            jnp.where(here, packed(part_ref.at[2 * i + quantity], start), zero).reshape(HALF, width)
            for i in range(3)
            for quantity in range(sent)
        ]
        total += dot(jnp.concatenate(parts, axis=0), hot, 1, 1)
    high, middle, low = (total[i * sent * HALF : (i + 1) * sent * HALF] for i in range(3))
    total = high + (middle + low)

    def unfold(values):
        return jnp.concatenate([values[:, :slots], values[:, slots:]], axis=0).T

    own = unfold(total[:HALF])
    send_ref[...] = own if sent == 1 else merge_pair(own, unfold(total[HALF:]))


def call(body, out_shape, *operands, scalars=0, scratch=()):
    vmem = pl.BlockSpec(memory_space=pltpu.VMEM)
    smem = pl.BlockSpec(memory_space=pltpu.SMEM)
    return pl.pallas_call(
        body,
        out_shape=out_shape,
        in_specs=[smem] * scalars + [vmem] * (len(operands) - scalars),
        out_specs=jax.tree.map(lambda _: vmem, out_shape),
        scratch_shapes=list(scratch),
        compiler_params=pltpu.CompilerParams(vmem_limit_bytes=VMEM_LIMIT),
    )(*operands)


def exchange(rows, peers):
    shape = (peers, rows.shape[0] // peers, LANES)
    return lax.all_to_all(rows.reshape(shape), GROUP, 0, 0, tiled=True).reshape(rows.shape)


def swap(values):
    side = lax.axis_size("sec")
    pairs = [(i * side + j, j * side + i) for i in range(side) for j in range(side)]
    return lax.ppermute(values, ("sec", "far"), pairs)


def shards(
    gas_field,
    parcel_state,
    parcel_mass,
    base_time,
    evap_rate,
    slot_blocks,
    parcel_block_slot,
    parcel_cell,
    parcel_count,
):
    along_x, pencils, along_z = gas_field.shape[1:]
    per_pencil = along_z // LANES
    blocks = along_x * pencils * per_pencil
    peers, per_peer = slot_blocks.shape[1:]
    slots = peers * per_peer
    lines = parcel_mass.shape[0] // LANES
    rows = 2 * slots

    def shape(dims, kind=F32):
        return jax.ShapeDtypeStruct(dims, kind)

    lists = swap(slot_blocks)
    own_gas = gas_field.reshape(along_x, pencils, per_pencil, LANES)
    own_gas = jnp.swapaxes(own_gas, 1, 2).reshape(blocks, LANES)
    own_drop = parcel_state.reshape(lines, LANES)
    together = lax.all_gather(
        jnp.concatenate([own_gas, own_drop], axis=0), "sec", axis=0, tiled=True
    )
    lists, together = lax.optimization_barrier((lists, together))
    wanted = call(
        functools.partial(order_kernel, pencils, per_pencil),
        shape((slots, LANES), BF16),
        lists,
    )
    wanted = exchange(wanted, peers)
    pack = call(
        functools.partial(pack_kernel, slots),
        shape((2 * blocks + 7 * lines, LANES)),
        parcel_count,
        together,
        own_gas,
        own_drop,
        *(
            part.reshape(lines, LANES)
            for part in (parcel_mass, base_time, evap_rate, parcel_block_slot, parcel_cell)
        ),
        scalars=1,
    )
    pack = swap(pack)

    gas_shape = shape((2 * blocks, LANES))
    send_shape = shape((rows, LANES), BF16)
    pick, place, own_place, send = call(
        pick_kernel,
        (
            shape((rows, 2 * blocks), BF16),
            shape((2 * blocks, rows), BF16),
            shape((blocks, slots), BF16),
            send_shape,
        ),
        wanted,
        pack,
    )
    gas, state = pack, ()
    for substep in range(ITERS):
        last = substep == ITERS - 1
        recv = exchange(send, peers)
        state, source = call(
            functools.partial(parcel_kernel, 4, substep == 0),
            (
                shape((2 if last else 3, lines, LANES)),
                shape((slots if last else rows, LANES)),
            ),
            recv,
            pack,
            *state,
            scratch=[pltpu.VMEM((2, lines, LANES), F32), pltpu.VMEM((6, lines, LANES), F32)],
        )
        source = exchange(source, peers)
        update = functools.partial(gas_kernel, pencils, per_pencil)
        if last:
            gas = call(update, shape((blocks, LANES)), source, gas, pick, own_place)
        else:
            gas, send = call(update, (gas_shape, send_shape), source, gas, pick, place)
            state = (state,)
    state = swap(state)
    gas = swap(gas).reshape(along_x, per_pencil, pencils, LANES)
    return (
        jnp.swapaxes(gas, 1, 2).reshape(gas_field.shape),
        state[OWN].reshape(parcel_state.shape),
        state[MASS].reshape(parcel_mass.shape),
    )


def solution(mesh):
    sec, row, col = (mesh.shape[name] for name in ("sec", "row", "col"))
    split = Mesh(mesh.devices.reshape(sec, row, sec, col // sec), ("sec", "row", "far", "near"))
    place = P(("row", "far", "near"))
    return jax.shard_map(
        shards,
        mesh=split,
        in_specs=(
            P("sec", "row", ("far", "near"), None),
            P("sec", ("row", "far", "near")),
            place,
            place,
            place,
            P(("row", "far", "near"), None, None),
            place,
            place,
            place,
        ),
        out_specs=(
            P("sec", "row", ("far", "near"), None),
            P("sec", ("row", "far", "near")),
            place,
        ),
        check_vma=False,
    )
```

```python
import functools

import jax
import jax.numpy as jnp
from jax import lax
from jax.experimental import pallas as pl
from jax.experimental.pallas import tpu as pltpu
from jax.sharding import Mesh
from jax.sharding import PartitionSpec as P

ITERS = 4
LATENT = 2.0
DEPOSIT_MODE = 0.5
ADVECT = 0.3
DIFFUSE = 0.2
LANES = 128
HALF = 64
GROUP = ("sec", "near")
OWN, MASS, TEMP, BASE, EVAP, SLOT, CELL = range(7)
VMEM_LIMIT = 32 * 1024 * 1024

F32 = jnp.float32
BF16 = jnp.bfloat16


def iota(shape, axis):
    return lax.broadcasted_iota(jnp.int32, shape, axis)


def dot(left_side, right_side, left_axis=1, right_axis=0):
    return lax.dot_general(
        left_side,
        right_side,
        (((left_axis,), (right_axis,)), ((), ())),
        preferred_element_type=F32,
    )


def thirds(values):
    high = values.astype(BF16).astype(F32)
    rest = values - high
    middle = rest.astype(BF16).astype(F32)
    return high, middle, rest - middle


def split_pair(rows):
    tiles = rows.reshape(rows.shape[0] // 16, 2, 8, LANES)
    even, odd = tiles[:, 0], tiles[:, 1]
    low = iota(even.shape, 1) < 4
    first = jnp.where(low, even, pltpu.roll(odd, 4, 1))
    second = jnp.where(low, pltpu.roll(even, 4, 1), odd)
    flat = (rows.shape[0] // 2, LANES)
    return first.reshape(flat), second.reshape(flat)


def merge_pair(first, second):
    shape = (first.shape[0] // 8, 8, LANES)
    first, second = first.reshape(shape), second.reshape(shape)
    low = iota(shape, 1) < 4
    even = jnp.where(low, first, pltpu.roll(second, 4, 1))
    odd = jnp.where(low, pltpu.roll(first, 4, 1), second)
    return jnp.stack([even, odd], axis=1).reshape(2 * shape[0] * 8, LANES)


def order_kernel(pencils, per_pencil, list_ref, rows_ref):
    block = list_ref[0]
    peers, per_peer = block.shape
    first = block // (pencils * per_pencil)
    rest = block - first * (pencils * per_pencil)
    pencil = rest // per_pencil
    line = first * (pencils * per_pencil) + (rest - pencil * per_pencil) * pencils + pencil
    slots = rows_ref.shape[0]
    owner = (iota((slots, peers), 0) // per_peer == iota((slots, peers), 1)).astype(BF16)
    spread = dot(owner, line.astype(F32).astype(BF16))
    mine = iota(spread.shape, 0) % per_peer == iota(spread.shape, 1)
    value = jnp.sum(jnp.where(mine, spread, 0.0), axis=1, keepdims=True)
    rows_ref[...] = jnp.broadcast_to(value, rows_ref.shape).astype(BF16)


def pack_kernel(
    slots, count_ref, temp_ref, gas_ref, drop_ref, mass_ref, base_ref, evap_ref, slot_ref, cell_ref,
    gas_out, out_ref,
):
    blocks, lines = gas_ref.shape[0], mass_ref.shape[0]
    start = temp_ref.shape[0] - blocks - lines
    gas_out[:blocks] = gas_ref[...]
    gas_out[blocks:] = temp_ref[start : start + blocks]

    def store(which, values):
        at = which * lines
        out_ref[at : at + lines] = values

    store(OWN, drop_ref[...])
    store(MASS, mass_ref[...])
    store(TEMP, temp_ref[start + blocks :])
    store(BASE, base_ref[...])
    store(EVAP, evap_ref[...])
    shape = mass_ref.shape
    active = iota(shape, 0) * LANES + iota(shape, 1) < count_ref[0]
    upper = cell_ref[...] // HALF
    store(SLOT, (slot_ref[...] + slots * upper).astype(F32))
    store(CELL, jnp.where(active, cell_ref[...] - HALF * upper, -1).astype(F32))


def pick_kernel(wanted_ref, pack_ref, pick_ref, place_ref, own_place_ref, send_ref):
    lines = wanted_ref[...].astype(F32)
    own = (lines == iota(lines.shape, 1).astype(F32)).astype(F32)
    own_place_ref[...] = own.T[: own_place_ref.shape[0]].astype(BF16)
    wanted = merge_pair(lines, lines + pick_ref.shape[1] / 2)
    pick = (wanted == iota(pick_ref.shape, 1).astype(F32)).astype(F32)
    pick_ref[...] = pick.astype(BF16)
    place_ref[...] = pick.T.astype(BF16)
    gas = pack_ref[: pick_ref.shape[1]]
    send_ref[...] = dot(pick.astype(BF16), gas.astype(BF16)).astype(BF16)


def gas_kernel(stride, per_pencil, source_ref, gas_ref, pick_ref, place_ref, gas_out, send_ref=None):
    place = place_ref[...]
    high, middle, low = (dot(place, part.astype(BF16)) for part in thirds(source_ref[...]))
    deposit = high + (middle + low)
    rows = place.shape[0]
    gas = gas_ref[:rows]
    block = iota(gas.shape, 0) // stride % per_pencil
    lane = iota(gas.shape, 1)
    to_right = pltpu.roll(gas, 1, 1)
    to_left = pltpu.roll(gas, LANES - 1, 1)
    left = jnp.where(
        lane == 0, jnp.where(block == 0, gas, pltpu.roll(to_right, stride, 0)), to_right
    )
    right = jnp.where(
        lane == LANES - 1,
        jnp.where(block == per_pencil - 1, gas, pltpu.roll(to_left, rows - stride, 0)),
        to_left,
    )
    moved = gas + ADVECT * (left - gas) + DIFFUSE * (right - 2.0 * gas + left)
    new_gas = moved + DEPOSIT_MODE * deposit
    gas_out[...] = new_gas[: gas_out.shape[0]]
    if send_ref is not None:
        send_ref[...] = dot(pick_ref[...], new_gas.astype(BF16)).astype(BF16)


def parcel_kernel(chunk, first, recv_ref, pack_ref, *refs):
    state_ref = None if first else refs[0]
    state_out, send_ref, seen_ref, part_ref = refs[-4:]
    lines = state_out.shape[1]
    base_row = pack_ref.shape[0] - 7 * lines
    slots = recv_ref.shape[0] // 2
    width = chunk * LANES

    def given(which):
        return pack_ref[base_row + which * lines : base_row + (which + 1) * lines]

    def held(which):
        return given(which) if first else state_ref[which]

    def fold(values):
        turned = values.T
        return jnp.concatenate([turned[:HALF], turned[HALF:]], axis=1)

    own, temp = split_pair(recv_ref[...].astype(F32))
    table = jnp.concatenate([fold(own), fold(temp)], axis=0).astype(BF16)

    def packed(ref, start):
        row = jnp.concatenate([ref[start + i : start + i + 1, :] for i in range(chunk)], axis=1)
        return jnp.broadcast_to(row, (16, width)).astype(BF16)[None]

    def index(count):
        shape = (count // 16, 16, width)
        return (iota(shape, 0) * 16 + iota(shape, 1)).astype(F32).astype(BF16)

    slot_index, cell_index = index(2 * slots), index(HALF)
    one, zero = jnp.ones((), BF16), jnp.zeros((), BF16)

    def masks(start):
        hot = jnp.where(slot_index == packed(pack_ref, base_row + SLOT * lines + start), one, zero)
        here = cell_index == packed(pack_ref, base_row + CELL * lines + start)
        return hot.reshape(2 * slots, width), here

    for start in range(0, lines, chunk):
        hot, here = masks(start)
        values = dot(table, hot).astype(BF16).reshape(2, HALF // 16, 16, width)
        for quantity in range(2):
            kept = jnp.where(here, values[quantity], zero)
            total = kept[0]
            for i in range(1, HALF // 16):
                total = total + kept[i]
            seen = jnp.sum(total.astype(F32), axis=0, keepdims=True)
            for i in range(chunk):
                seen_ref[quantity, start + i : start + i + 1, :] = seen[:, i * LANES : (i + 1) * LANES]

    hot_quantity = lax.axis_index("far") == 3
    own_heat = jnp.where(hot_quantity, 1.5, 1.0).astype(F32)
    own_latent = jnp.where(hot_quantity, LATENT, 0.0).astype(F32)
    active = given(CELL) >= 0.0
    mass = held(MASS)
    evap_now = given(EVAP) * jax.nn.sigmoid(seen_ref[1] - held(TEMP))
    new_mass = jnp.where(active, mass * jnp.exp(-evap_now), mass)
    state_out[MASS] = new_mass
    unit_time = given(BASE) * jnp.exp(jnp.log(mass) * (2.0 / 3.0))
    work = ((OWN, own_heat, own_latent), (TEMP, 1.5, LATENT))
    for quantity, (which, heat, latent) in enumerate(work):
        seen, drop = seen_ref[quantity], held(which)
        relaxed = seen + (drop - seen) * jnp.exp(-1.0 / (unit_time * heat))
        new_drop = jnp.where(active, relaxed, drop)
        if which < state_out.shape[0]:
            state_out[which] = new_drop
        source = mass * drop - new_mass * new_drop - latent * (mass - new_mass)
        for i, part in enumerate(thirds(source)):
            part_ref[2 * i + quantity] = part

    sent = 2 if state_out.shape[0] > TEMP else 1
    total = jnp.zeros((3 * sent * HALF, 2 * slots), F32)
    for start in range(0, lines, chunk):
        hot, here = masks(start)
        parts = [
            jnp.where(here, packed(part_ref.at[2 * i + quantity], start), zero).reshape(HALF, width)
            for i in range(3)
            for quantity in range(sent)
        ]
        total += dot(jnp.concatenate(parts, axis=0), hot, 1, 1)
    high, middle, low = (total[i * sent * HALF : (i + 1) * sent * HALF] for i in range(3))
    total = high + (middle + low)

    def unfold(values):
        return jnp.concatenate([values[:, :slots], values[:, slots:]], axis=0).T

    own = unfold(total[:HALF])
    send_ref[...] = own if sent == 1 else merge_pair(own, unfold(total[HALF:]))


def call(body, out_shape, *operands, scalars=0, scratch=()):
    vmem = pl.BlockSpec(memory_space=pltpu.VMEM)
    smem = pl.BlockSpec(memory_space=pltpu.SMEM)
    return pl.pallas_call(
        body,
        out_shape=out_shape,
        in_specs=[smem] * scalars + [vmem] * (len(operands) - scalars),
        out_specs=jax.tree.map(lambda _: vmem, out_shape),
        scratch_shapes=list(scratch),
        compiler_params=pltpu.CompilerParams(vmem_limit_bytes=VMEM_LIMIT),
    )(*operands)


def exchange(rows, peers):
    shape = (peers, rows.shape[0] // peers, LANES)
    return lax.all_to_all(rows.reshape(shape), GROUP, 0, 0, tiled=True).reshape(rows.shape)


def swap(values):
    side = lax.axis_size("sec")
    pairs = [(i * side + j, j * side + i) for i in range(side) for j in range(side)]
    return lax.ppermute(values, ("sec", "far"), pairs)


def shards(
    gas_field,
    parcel_state,
    parcel_mass,
    base_time,
    evap_rate,
    slot_blocks,
    parcel_block_slot,
    parcel_cell,
    parcel_count,
):
    along_x, pencils, along_z = gas_field.shape[1:]
    per_pencil = along_z // LANES
    blocks = along_x * pencils * per_pencil
    peers, per_peer = slot_blocks.shape[1:]
    slots = peers * per_peer
    lines = parcel_mass.shape[0] // LANES
    rows = 2 * slots

    def shape(dims, kind=F32):
        return jax.ShapeDtypeStruct(dims, kind)

    lists = swap(slot_blocks)
    own_gas = gas_field.reshape(along_x, pencils, per_pencil, LANES)
    own_gas = jnp.swapaxes(own_gas, 1, 2).reshape(blocks, LANES)
    own_drop = parcel_state.reshape(lines, LANES)
    together = lax.all_gather(
        jnp.concatenate([own_gas, own_drop], axis=0), "sec", axis=0, tiled=True
    )
    lists, together = lax.optimization_barrier((lists, together))
    wanted = call(
        functools.partial(order_kernel, pencils, per_pencil),
        shape((slots, LANES), BF16),
        lists,
    )
    wanted = exchange(wanted, peers)
    gas, pack = call(
        functools.partial(pack_kernel, slots),
        (shape((2 * blocks, LANES)), shape((7 * lines, LANES))),
        parcel_count,
        together,
        own_gas,
        own_drop,
        *(
            part.reshape(lines, LANES)
            for part in (parcel_mass, base_time, evap_rate, parcel_block_slot, parcel_cell)
        ),
        scalars=1,
    )
    gas = swap(gas)

    gas_shape = shape((2 * blocks, LANES))
    send_shape = shape((rows, LANES), BF16)
    pick, place, own_place, send = call(
        pick_kernel,
        (
            shape((rows, 2 * blocks), BF16),
            shape((2 * blocks, rows), BF16),
            shape((blocks, slots), BF16),
            send_shape,
        ),
        wanted,
        gas,
    )
    pack, send = lax.optimization_barrier((pack, send))
    pack = swap(pack)
    state = ()
    for substep in range(ITERS):
        last = substep == ITERS - 1
        recv = exchange(send, peers)
        state, source = call(
            functools.partial(parcel_kernel, 4, substep == 0),
            (
                shape((2 if last else 3, lines, LANES)),
                shape((slots if last else rows, LANES)),
            ),
            recv,
            pack,
            *state,
            scratch=[pltpu.VMEM((2, lines, LANES), F32), pltpu.VMEM((6, lines, LANES), F32)],
        )
        source = exchange(source, peers)
        update = functools.partial(gas_kernel, pencils, per_pencil)
        if last:
            gas = call(update, shape((blocks, LANES)), source, gas, pick, own_place)
        else:
            gas, send = call(update, (gas_shape, send_shape), source, gas, pick, place)
            state = (state,)
    state = swap(state)
    gas = swap(gas).reshape(along_x, per_pencil, pencils, LANES)
    return (
        jnp.swapaxes(gas, 1, 2).reshape(gas_field.shape),
        state[OWN].reshape(parcel_state.shape),
        state[MASS].reshape(parcel_mass.shape),
    )


def solution(mesh):
    sec, row, col = (mesh.shape[name] for name in ("sec", "row", "col"))
    split = Mesh(mesh.devices.reshape(sec, row, sec, col // sec), ("sec", "row", "far", "near"))
    place = P(("row", "far", "near"))
    return jax.shard_map(
        shards,
        mesh=split,
        in_specs=(
            P("sec", "row", ("far", "near"), None),
            P("sec", ("row", "far", "near")),
            place,
            place,
            place,
            P(("row", "far", "near"), None, None),
            place,
            place,
            place,
        ),
        out_specs=(
            P("sec", "row", ("far", "near"), None),
            P("sec", ("row", "far", "near")),
            place,
        ),
        check_vma=False,
    )
```

```python
import functools

import jax
import jax.numpy as jnp
from jax import lax
from jax.experimental import pallas as pl
from jax.experimental.pallas import tpu as pltpu
from jax.sharding import Mesh
from jax.sharding import PartitionSpec as P

ITERS = 4
LATENT = 2.0
DEPOSIT_MODE = 0.5
ADVECT = 0.3
DIFFUSE = 0.2
LANES = 128
HALF = 64
GROUP = ("sec", "near")
OWN, MASS, TEMP, BASE, EVAP, SLOT, CELL = range(7)
VMEM_LIMIT = 32 * 1024 * 1024

F32 = jnp.float32
BF16 = jnp.bfloat16


def iota(shape, axis):
    return lax.broadcasted_iota(jnp.int32, shape, axis)


def dot(left_side, right_side, left_axis=1, right_axis=0):
    return lax.dot_general(
        left_side,
        right_side,
        (((left_axis,), (right_axis,)), ((), ())),
        preferred_element_type=F32,
    )


def thirds(values):
    high = values.astype(BF16).astype(F32)
    rest = values - high
    middle = rest.astype(BF16).astype(F32)
    return high, middle, rest - middle


def split_pair(rows):
    tiles = rows.reshape(rows.shape[0] // 16, 2, 8, LANES)
    even, odd = tiles[:, 0], tiles[:, 1]
    low = iota(even.shape, 1) < 4
    first = jnp.where(low, even, pltpu.roll(odd, 4, 1))
    second = jnp.where(low, pltpu.roll(even, 4, 1), odd)
    flat = (rows.shape[0] // 2, LANES)
    return first.reshape(flat), second.reshape(flat)


def merge_pair(first, second):
    shape = (first.shape[0] // 8, 8, LANES)
    first, second = first.reshape(shape), second.reshape(shape)
    low = iota(shape, 1) < 4
    even = jnp.where(low, first, pltpu.roll(second, 4, 1))
    odd = jnp.where(low, pltpu.roll(first, 4, 1), second)
    return jnp.stack([even, odd], axis=1).reshape(2 * shape[0] * 8, LANES)


def order_kernel(pencils, per_pencil, list_ref, rows_ref):
    block = list_ref[0]
    peers, per_peer = block.shape
    first = block // (pencils * per_pencil)
    rest = block - first * (pencils * per_pencil)
    pencil = rest // per_pencil
    line = first * (pencils * per_pencil) + (rest - pencil * per_pencil) * pencils + pencil
    slots = rows_ref.shape[0]
    owner = (iota((slots, peers), 0) // per_peer == iota((slots, peers), 1)).astype(BF16)
    spread = dot(owner, line.astype(F32).astype(BF16))
    mine = iota(spread.shape, 0) % per_peer == iota(spread.shape, 1)
    value = jnp.sum(jnp.where(mine, spread, 0.0), axis=1, keepdims=True)
    rows_ref[...] = jnp.broadcast_to(value, rows_ref.shape).astype(BF16)


def pack_kernel(
    slots, count_ref, temp_ref, gas_ref, drop_ref, mass_ref, base_ref, evap_ref, slot_ref, cell_ref, out_ref
):
    blocks, lines = gas_ref.shape[0], mass_ref.shape[0]
    start = temp_ref.shape[0] - blocks - lines
    out_ref[:blocks] = gas_ref[...]
    out_ref[blocks : 2 * blocks] = temp_ref[start : start + blocks]

    def store(which, values):
        at = 2 * blocks + which * lines
        out_ref[at : at + lines] = values

    store(OWN, drop_ref[...])
    store(MASS, mass_ref[...])
    store(TEMP, temp_ref[start + blocks :])
    store(BASE, base_ref[...])
    store(EVAP, evap_ref[...])
    shape = mass_ref.shape
    active = iota(shape, 0) * LANES + iota(shape, 1) < count_ref[0]
    upper = cell_ref[...] // HALF
    store(SLOT, (slot_ref[...] + slots * upper).astype(F32))
    store(CELL, jnp.where(active, cell_ref[...] - HALF * upper, -1).astype(F32))


def pick_kernel(wanted_ref, pack_ref, pick_ref, place_ref, own_place_ref, send_ref):
    lines = wanted_ref[...].astype(F32)
    own = (lines == iota(lines.shape, 1).astype(F32)).astype(F32)
    own_place_ref[...] = own.T[: own_place_ref.shape[0]].astype(BF16)
    wanted = merge_pair(lines, lines + pick_ref.shape[1] / 2)
    pick = (wanted == iota(pick_ref.shape, 1).astype(F32)).astype(F32)
    pick_ref[...] = pick.astype(BF16)
    place_ref[...] = pick.T.astype(BF16)
    gas = pack_ref[: pick_ref.shape[1]]
    send_ref[...] = dot(pick.astype(BF16), gas.astype(BF16)).astype(BF16)


def gas_kernel(stride, per_pencil, source_ref, gas_ref, pick_ref, place_ref, gas_out, send_ref=None):
    place = place_ref[...]
    high, middle, low = (dot(place, part.astype(BF16)) for part in thirds(source_ref[...]))
    deposit = high + (middle + low)
    rows = place.shape[0]
    gas = gas_ref[:rows]
    block = iota(gas.shape, 0) // stride % per_pencil
    lane = iota(gas.shape, 1)
    to_right = pltpu.roll(gas, 1, 1)
    to_left = pltpu.roll(gas, LANES - 1, 1)
    left = jnp.where(
        lane == 0, jnp.where(block == 0, gas, pltpu.roll(to_right, stride, 0)), to_right
    )
    right = jnp.where(
        lane == LANES - 1,
        jnp.where(block == per_pencil - 1, gas, pltpu.roll(to_left, rows - stride, 0)),
        to_left,
    )
    moved = gas + ADVECT * (left - gas) + DIFFUSE * (right - 2.0 * gas + left)
    new_gas = moved + DEPOSIT_MODE * deposit
    gas_out[...] = new_gas[: gas_out.shape[0]]
    if send_ref is not None:
        send_ref[...] = dot(pick_ref[...], new_gas.astype(BF16)).astype(BF16)


def parcel_kernel(chunk, first, recv_ref, pack_ref, *refs):
    state_ref = None if first else refs[0]
    state_out, send_ref, seen_ref, part_ref = refs[-4:]
    lines = state_out.shape[1]
    base_row = pack_ref.shape[0] - 7 * lines
    slots = recv_ref.shape[0] // 2
    width = chunk * LANES

    def given(which):
        return pack_ref[base_row + which * lines : base_row + (which + 1) * lines]

    def held(which):
        return given(which) if first else state_ref[which]

    def fold(values):
        turned = values.T
        return jnp.concatenate([turned[:HALF], turned[HALF:]], axis=1)

    own, temp = split_pair(recv_ref[...].astype(F32))
    table = jnp.concatenate([fold(own), fold(temp)], axis=0).astype(BF16)

    def packed(ref, start):
        row = jnp.concatenate([ref[start + i : start + i + 1, :] for i in range(chunk)], axis=1)
        return jnp.broadcast_to(row, (16, width)).astype(BF16)[None]

    def index(count):
        shape = (count // 16, 16, width)
        return (iota(shape, 0) * 16 + iota(shape, 1)).astype(F32).astype(BF16)

    slot_index, cell_index = index(2 * slots), index(HALF)
    one, zero = jnp.ones((), BF16), jnp.zeros((), BF16)

    def masks(start):
        hot = jnp.where(slot_index == packed(pack_ref, base_row + SLOT * lines + start), one, zero)
        here = cell_index == packed(pack_ref, base_row + CELL * lines + start)
        return hot.reshape(2 * slots, width), here

    for start in range(0, lines, chunk):
        hot, here = masks(start)
        values = dot(table, hot).astype(BF16).reshape(2, HALF // 16, 16, width)
        for quantity in range(2):
            kept = jnp.where(here, values[quantity], zero)
            total = kept[0]
            for i in range(1, HALF // 16):
                total = total + kept[i]
            seen = jnp.sum(total.astype(F32), axis=0, keepdims=True)
            for i in range(chunk):
                seen_ref[quantity, start + i : start + i + 1, :] = seen[:, i * LANES : (i + 1) * LANES]

    hot_quantity = lax.axis_index("far") == 3
    own_heat = jnp.where(hot_quantity, 1.5, 1.0).astype(F32)
    own_latent = jnp.where(hot_quantity, LATENT, 0.0).astype(F32)
    active = given(CELL) >= 0.0
    mass = held(MASS)
    evap_now = given(EVAP) * jax.nn.sigmoid(seen_ref[1] - held(TEMP))
    new_mass = jnp.where(active, mass * jnp.exp(-evap_now), mass)
    state_out[MASS] = new_mass
    unit_time = given(BASE) * jnp.exp(jnp.log(mass) * (2.0 / 3.0))
    work = ((OWN, own_heat, own_latent), (TEMP, 1.5, LATENT))
    for quantity, (which, heat, latent) in enumerate(work):
        seen, drop = seen_ref[quantity], held(which)
        relaxed = seen + (drop - seen) * jnp.exp(-1.0 / (unit_time * heat))
        new_drop = jnp.where(active, relaxed, drop)
        if which < state_out.shape[0]:
            state_out[which] = new_drop
        source = mass * drop - new_mass * new_drop - latent * (mass - new_mass)
        for i, part in enumerate(thirds(source)):
            part_ref[2 * i + quantity] = part

    sent = 2 if state_out.shape[0] > TEMP else 1
    total = jnp.zeros((3 * sent * HALF, 2 * slots), F32)
    for start in range(0, lines, chunk):
        hot, here = masks(start)
        parts = [
            jnp.where(here, packed(part_ref.at[2 * i + quantity], start), zero).reshape(HALF, width)
            for i in range(3)
            for quantity in range(sent)
        ]
        total += dot(jnp.concatenate(parts, axis=0), hot, 1, 1)
    high, middle, low = (total[i * sent * HALF : (i + 1) * sent * HALF] for i in range(3))
    total = high + (middle + low)

    def unfold(values):
        return jnp.concatenate([values[:, :slots], values[:, slots:]], axis=0).T

    own = unfold(total[:HALF])
    send_ref[...] = own if sent == 1 else merge_pair(own, unfold(total[HALF:]))


def call(body, out_shape, *operands, scalars=0, scratch=()):
    vmem = pl.BlockSpec(memory_space=pltpu.VMEM)
    smem = pl.BlockSpec(memory_space=pltpu.SMEM)
    return pl.pallas_call(
        body,
        out_shape=out_shape,
        in_specs=[smem] * scalars + [vmem] * (len(operands) - scalars),
        out_specs=jax.tree.map(lambda _: vmem, out_shape),
        scratch_shapes=list(scratch),
        compiler_params=pltpu.CompilerParams(vmem_limit_bytes=VMEM_LIMIT),
    )(*operands)


def exchange(rows, peers):
    shape = (peers, rows.shape[0] // peers, LANES)
    return lax.all_to_all(rows.reshape(shape), GROUP, 0, 0, tiled=True).reshape(rows.shape)


def swap(values):
    side = lax.axis_size("sec")
    pairs = [(i * side + j, j * side + i) for i in range(side) for j in range(side)]
    return lax.ppermute(values, ("sec", "far"), pairs)


def shards(
    gas_field,
    parcel_state,
    parcel_mass,
    base_time,
    evap_rate,
    slot_blocks,
    parcel_block_slot,
    parcel_cell,
    parcel_count,
):
    along_x, pencils, along_z = gas_field.shape[1:]
    per_pencil = along_z // LANES
    blocks = along_x * pencils * per_pencil
    peers, per_peer = slot_blocks.shape[1:]
    slots = peers * per_peer
    lines = parcel_mass.shape[0] // LANES
    rows = 2 * slots

    def shape(dims, kind=F32):
        return jax.ShapeDtypeStruct(dims, kind)

    lists = swap(slot_blocks)
    own_gas = gas_field.reshape(along_x, pencils, per_pencil, LANES)
    own_gas = jnp.swapaxes(own_gas, 1, 2).reshape(blocks, LANES)
    own_drop = parcel_state.reshape(lines, LANES)
    together = lax.all_gather(
        jnp.concatenate([own_gas, own_drop], axis=0), "sec", axis=0, tiled=True
    )
    lists, together = lax.optimization_barrier((lists, together))
    wanted = call(
        functools.partial(order_kernel, pencils, per_pencil),
        shape((slots, LANES), BF16),
        lists,
    )
    wanted = exchange(wanted, peers)
    pack = call(
        functools.partial(pack_kernel, slots),
        shape((2 * blocks + 7 * lines, LANES)),
        parcel_count,
        together,
        own_gas,
        own_drop,
        *(
            part.reshape(lines, LANES)
            for part in (parcel_mass, base_time, evap_rate, parcel_block_slot, parcel_cell)
        ),
        scalars=1,
    )
    pack = swap(pack)

    gas_shape = shape((2 * blocks, LANES))
    send_shape = shape((rows, LANES), BF16)
    pick, place, own_place, send = call(
        pick_kernel,
        (
            shape((rows, 2 * blocks), BF16),
            shape((2 * blocks, rows), BF16),
            shape((blocks, slots), BF16),
            send_shape,
        ),
        wanted,
        pack,
    )
    gas, state = pack, ()
    for substep in range(ITERS):
        last = substep == ITERS - 1
        recv = exchange(send, peers)
        state, source = call(
            functools.partial(parcel_kernel, 4, substep == 0),
            (
                shape((2 if last else 3, lines, LANES)),
                shape((slots if last else rows, LANES)),
            ),
            recv,
            pack,
            *state,
            scratch=[pltpu.VMEM((2, lines, LANES), F32), pltpu.VMEM((6, lines, LANES), F32)],
        )
        source = exchange(source, peers)
        update = functools.partial(gas_kernel, pencils, per_pencil)
        if last:
            gas = call(update, shape((blocks, LANES)), source, gas, pick, own_place)
        else:
            gas, send = call(update, (gas_shape, send_shape), source, gas, pick, place)
            state = (state,)
    gas, state = lax.optimization_barrier((gas, state))
    both = swap(jnp.concatenate([gas, state.reshape(2 * lines, LANES)], axis=0))
    gas, state = both[:blocks], both[blocks:].reshape(2, lines, LANES)
    gas = gas.reshape(along_x, per_pencil, pencils, LANES)
    return (
        jnp.swapaxes(gas, 1, 2).reshape(gas_field.shape),
        state[OWN].reshape(parcel_state.shape),
        state[MASS].reshape(parcel_mass.shape),
    )


def solution(mesh):
    sec, row, col = (mesh.shape[name] for name in ("sec", "row", "col"))
    split = Mesh(mesh.devices.reshape(sec, row, sec, col // sec), ("sec", "row", "far", "near"))
    place = P(("row", "far", "near"))
    return jax.shard_map(
        shards,
        mesh=split,
        in_specs=(
            P("sec", "row", ("far", "near"), None),
            P("sec", ("row", "far", "near")),
            place,
            place,
            place,
            P(("row", "far", "near"), None, None),
            place,
            place,
            place,
        ),
        out_specs=(
            P("sec", "row", ("far", "near"), None),
            P("sec", ("row", "far", "near")),
            place,
        ),
        check_vma=False,
    )
```
